32 devices in a mesh: ha: 16 (over z, x, core), wa: 2 (over y).
Axes of the slice: x: 2, y: 2, z: 4, core: 2. Of those that a mesh axis runs over, the one named last changes fastest.
Arguments:
- queries: bfloat16 [256, 128, 384], P('ha', 'wa'), may hold values from -200 to 200
- key_tokens: bfloat16 [256, 128, 384], P('ha', 'wa'), may hold values from -6 to 6
- value_tokens: bfloat16 [256, 128, 384], P('ha', 'wa'), may hold values from -6 to 6
- out_grad: bfloat16 [256, 128, 384], P('ha', 'wa'), may hold values from -96 to 96
- key_kernel: bfloat16 [3, 3, 384], replicated, may hold values from -2 to 2
- value_kernel: bfloat16 [3, 3, 384], replicated, may hold values from -2 to 2
- height_table: bfloat16 [511, 96], replicated, may hold values from -0.8984375 to 0.8984375
- width_table: bfloat16 [255, 96], replicated, may hold values from -0.8984375 to 0.8984375
Outputs:
- query_grad: bfloat16 [256, 128, 384], P('ha', 'wa')
- key_grad: bfloat16 [256, 128, 384], P('ha', 'wa')
- value_grad: bfloat16 [256, 128, 384], P('ha', 'wa')
- height_grad: float32 [511, 96], replicated
- width_grad: float32 [255, 96], replicated
The draws below stay inside these ranges and needn't reach their ends.
All inputs are finite; a program needn't handle non-finite values.
Results may differ from the reference program's by a relative error of at most 0.02.
The reference program's roundings to bfloat16 on the way (of `key_pooled`, `height_rows`, `probs_low` and `grad_low`) count: a program that leaves them out, or rounds other values in their place, can miss the bound.
Values may be sent and summed in bfloat16 or wider, within the bound.
A program may use at most 128 MiB of HBM per device.

```python
import jax
import jax.numpy as jnp
from jax import lax

HEADS = 4
HD = 96
C = 384
KS = 3
STRIDE = 16
RH = 16
H = 256
W = 128
PH = 16
PW = 8
KEYS = 128
TH = 511
TW = 255
N_HA = 16


def draw_queries(key, part):
    first_key = jax.random.fold_in(key, 0)
    values = jnp.clip(jax.random.normal(first_key, (H, W, HEADS * HD), jnp.float32), -5.0, 5.0)
    return values.astype(jnp.bfloat16)


def steps_of(rng, dims, shards, least, largest):
    def one(axis_at, blocks):
        draws = jax.random.uniform(jax.random.fold_in(jax.random.fold_in(rng, 6), axis_at), (blocks,), jnp.float32, least / len(shards), largest / len(shards))
        return jnp.repeat(jnp.exp(draws), dims[axis_at] // blocks).reshape((-1,) + (1,) * (len(dims) - axis_at - 1))

    loudness = one(*shards[0])
    for cut in shards[1:]:
        loudness = loudness * one(*cut)
    return loudness


def normal_values(own_key, shape, spread, reach, cuts=(), kind=jnp.bfloat16):
    loudness = steps_of(own_key, shape, cuts, -0.22, 0.18) if cuts else 1.0
    entries = jax.random.normal(own_key, shape, jnp.float32) * spread * loudness
    return jnp.minimum(jnp.maximum(entries, -reach), reach).astype(kind)


def setup_inputs(seed: int = 0) -> dict:
    seeds = jax.random.split(jax.random.key(seed), 9)
    return {
        "queries": draw_queries(jax.random.fold_in(seeds[8], 71), 0),
        "key_tokens": normal_values(seeds[1], (H, W, C), 1.0, 6.0, ((0, 16), (1, 2))),
        "value_tokens": normal_values(seeds[2], (H, W, C), 1.0, 6.0, ((0, 16), (1, 2))),
        "out_grad": normal_values(seeds[3], (H, W, C), 16.0, 96.0, ((0, 16), (1, 2))),
        "key_kernel": normal_values(seeds[4], (KS, KS, C), (KS * KS) ** -0.5, 2.0),
        "value_kernel": normal_values(seeds[5], (KS, KS, C), (KS * KS) ** -0.5, 2.0),
        "height_table": normal_values(seeds[6], (TH, HD), 0.15, 0.8984375),
        "width_table": normal_values(seeds[7], (TW, HD), 0.15, 0.8984375),
    }


highest = lax.Precision.HIGHEST

def pool_global(tokens, kernel):
    halfwidth = KS // 2
    pooled = lax.conv_general_dilated(tokens.astype(jnp.float32)[None], kernel.astype(jnp.float32)[:, :, None, :], (STRIDE, STRIDE), ((halfwidth, halfwidth), (halfwidth, halfwidth)), dimension_numbers=('NHWC', 'HWIO', 'NHWC'), feature_group_count=tokens.shape[-1], precision=highest)
    return pooled[0]

def rounded(values):
    return lax.optimization_barrier(values.astype(jnp.bfloat16)).astype(jnp.float32)

def reference(queries, key_tokens, value_tokens, out_grad, key_kernel, value_kernel, height_table, width_table):
    score_scale = HD ** (-0.5)
    key_pooled = rounded(pool_global(key_tokens, key_kernel)).reshape(KEYS, HEADS, HD)
    value_pooled = rounded(pool_global(value_tokens, value_kernel)).reshape(KEYS, HEADS, HD)
    height_dist = (jnp.arange(H)[:, None] - STRIDE * jnp.arange(PH)[None, :] + (PH - 1) * STRIDE).astype(jnp.int32)
    width_dist = (jnp.arange(W)[:, None] - STRIDE * jnp.arange(PW)[None, :] + (PW - 1) * STRIDE).astype(jnp.int32)
    height_rows = height_table[height_dist].astype(jnp.float32)
    width_rows = width_table[width_dist].astype(jnp.float32)

    def block_step(totals, block_index):
        key_acc, value_acc, height_acc, width_acc = totals
        first_row = (block_index * RH).astype(jnp.int32)
        query_block = lax.dynamic_slice_in_dim(queries, first_row, RH, 0).astype(jnp.float32).reshape(RH, W, HEADS, HD)
        grad_block = lax.dynamic_slice_in_dim(out_grad, first_row, RH, 0).astype(jnp.float32).reshape(RH, W, HEADS, HD)
        height_block = lax.dynamic_slice_in_dim(height_rows, first_row, RH, 0)
        dist_block = lax.dynamic_slice_in_dim(height_dist, first_row, RH, 0)
        rel_height = jnp.einsum('rwnd,rkd->rwnk', query_block, height_block, precision=highest)
        rel_width = jnp.einsum('rwnd,wkd->rwnk', query_block, width_rows, precision=highest)
        score_bias = (rel_height[..., :, None] + rel_width[..., None, :]).reshape(RH * W, HEADS, KEYS)
        query_flat = query_block.reshape(RH * W, HEADS, HD)
        grad_flat = grad_block.reshape(RH * W, HEADS, HD)
        scores = score_scale * jnp.einsum('tnd,knd->tnk', query_flat, key_pooled, precision=highest) + score_bias
        scores = scores - lax.optimization_barrier(jnp.max(scores, axis=-1, keepdims=True))
        weights = jnp.exp(scores)
        attention = weights / lax.optimization_barrier(jnp.sum(weights, axis=-1, keepdims=True))
        probs_low = rounded(attention)
        attended = jnp.einsum('tnk,knd->tnd', probs_low, value_pooled, precision=highest)
        grad_probs = jnp.einsum('tnd,knd->tnk', grad_flat, value_pooled, precision=highest)
        row_delta = lax.optimization_barrier(jnp.sum(grad_flat * attended, axis=-1, keepdims=True))
        grad_scores = attention * (grad_probs - row_delta)
        grad_low = rounded(grad_scores)
        query_attn = score_scale * jnp.einsum('tnk,knd->tnd', grad_low, key_pooled, precision=highest)
        key_acc = key_acc + score_scale * jnp.einsum('tnk,tnd->knd', grad_low, query_flat, precision=highest)
        value_acc = value_acc + jnp.einsum('tnk,tnd->knd', probs_low, grad_flat, precision=highest)
        score_grid = grad_scores.reshape(RH, W, HEADS, PH, PW)
        grad_height = lax.optimization_barrier(jnp.sum(score_grid, axis=-1))
        grad_width = lax.optimization_barrier(jnp.sum(score_grid, axis=-2))
        query_rel = jnp.einsum('rwnk,rkd->rwnd', grad_height, height_block, precision=highest) + jnp.einsum('rwnk,wkd->rwnd', grad_width, width_rows, precision=highest)
        query_grad = (query_attn.reshape(RH, W, HEADS, HD) + query_rel).reshape(RH, W, HEADS * HD).astype(jnp.bfloat16)
        height_acc = height_acc.at[dist_block].add(jnp.einsum('rwnk,rwnd->rkd', grad_height, query_block, precision=highest))
        width_acc = width_acc.at[width_dist].add(jnp.einsum('rwnk,rwnd->wkd', grad_width, query_block, precision=highest))
        return ((key_acc, value_acc, height_acc, width_acc), query_grad)
    initial = (jnp.zeros((KEYS, HEADS, HD), jnp.float32), jnp.zeros((KEYS, HEADS, HD), jnp.float32), jnp.zeros((TH, HD), jnp.float32), jnp.zeros((TW, HD), jnp.float32))
    totals, blocks = lax.scan(block_step, initial, jnp.arange(N_HA))
    key_acc, value_acc, height_acc, width_acc = totals
    query_grad = blocks.reshape(H, W, HEADS * HD)
    _, key_back = jax.vjp(lambda tokens: pool_global(tokens, key_kernel), key_tokens.astype(jnp.float32))
    key_grad = key_back(key_acc.reshape(PH, PW, HEADS * HD))[0].astype(jnp.bfloat16)
    _, value_back = jax.vjp(lambda tokens: pool_global(tokens, value_kernel), value_tokens.astype(jnp.float32))
    value_grad = value_back(value_acc.reshape(PH, PW, HEADS * HD))[0].astype(jnp.bfloat16)
    return (query_grad, key_grad, value_grad, height_acc, width_acc)
```

```python
import functools

import jax
import jax.numpy as jnp
from jax import lax
from jax.experimental import pallas as pl
from jax.experimental.pallas import tpu as pltpu
from jax.sharding import PartitionSpec as P

HEADS = 4
HD = 96
KS = 3
STRIDE = 16
MESH = pl.DeviceIdType.MESH
F32 = jnp.float32
BF16 = jnp.bfloat16


def round_up(value, unit):
    return -(-value // unit) * unit


def greet(to_each, count):
    barrier = pltpu.get_barrier_semaphore()
    to_each(lambda device: pl.semaphore_signal(barrier, 1, device_id=device, device_id_type=MESH))
    pl.semaphore_wait(barrier, count)


def gather_kernel(
    n_ha, n_wa, pc,
    key_hbm, value_hbm, key_kernel, value_kernel, gathered,
    tokens, part, arrived, load_sem, own_send, own_recv, next_send, next_recv, row_send, row_recv,
):
    r = lax.axis_index("ha")
    w = lax.axis_index("wa")
    span = part.shape[2]
    kc = pc * n_wa
    last = tokens.shape[2] // pc
    has_next = r + 1 < n_ha
    has_prev = r > 0

    loads = []
    for a, source in enumerate((key_hbm, value_hbm)):
        loads.append(
            pltpu.make_async_copy(
                source.at[pl.ds(0, 2)], tokens.at[a, pl.ds(0, 2)], load_sem.at[2 * a]
            )
        )
        loads.append(
            pltpu.make_async_copy(
                source.at[pl.ds(STRIDE - 1, 1)], tokens.at[a, pl.ds(2, 1)], load_sem.at[2 * a + 1]
            )
        )
    for load in loads:
        load.start()

    barrier = pltpu.get_barrier_semaphore()

    @pl.loop(1, n_ha)
    def _(d):
        pl.semaphore_signal(
            barrier, 1, device_id=(lax.rem(r + d, n_ha), w), device_id_type=MESH
        )

    for d in range(1, n_wa):
        other = lax.rem(w + d, n_wa)
        pl.semaphore_signal(barrier, 1, device_id=(r, other), device_id_type=MESH)

        @pl.when(has_next)
        def _():
            pl.semaphore_signal(barrier, 1, device_id=(r + 1, other), device_id_type=MESH)

        @pl.when(has_prev)
        def _():
            pl.semaphore_signal(barrier, 1, device_id=(r - 1, other), device_id_type=MESH)

    extra = jnp.where(has_next, n_wa - 1, 0) + jnp.where(has_prev, n_wa - 1, 0)

    for load in loads:
        load.wait()

    def pooled(a, kernel, uses):
        rows = [None] * (pc + 1)

        def add(k, term):
            rows[k] = term if rows[k] is None else rows[k] + term

        for at, tap in uses:
            line = tokens[a, at].astype(F32)
            for k in range(pc):
                for col, to, key in ((0, 1, k), (1, 2, k), (STRIDE - 1, 0, k + 1)):
                    at_col = STRIDE * k + col
                    weight = kernel[tap, to : to + 1].astype(F32)
                    add(key, line[at_col : at_col + 1] * weight)
        return jnp.concatenate(
            rows + [jnp.zeros((span - pc - 1, tokens.shape[-1]), F32)], 0
        )

    for a, kernel in enumerate((key_kernel, value_kernel)):
        part[0, a] = pooled(a, kernel, ((0, 1), (1, 2)))
        part[1, a] = pooled(a, kernel, ((2, 0),))

    pl.semaphore_wait(barrier, n_ha - 1 + n_wa - 1 + extra)

    def own_copy(target, slot):
        return pltpu.make_async_remote_copy(
            src_ref=part.at[0],
            dst_ref=arrived.at[0, slot],
            send_sem=own_send.at[target],
            recv_sem=own_recv.at[slot],
            device_id=(r, target),
            device_id_type=MESH,
        )

    def next_copy(target, slot):
        return pltpu.make_async_remote_copy(
            src_ref=part.at[1],
            dst_ref=arrived.at[1, slot],
            send_sem=next_send.at[target],
            recv_sem=next_recv.at[slot],
            device_id=(r + 1, target),
            device_id_type=MESH,
        )

    for d in range(1, n_wa):
        own_copy(lax.rem(w + d, n_wa), w).start()

    @pl.when(has_next)
    def _():
        for d in range(n_wa):
            next_copy(lax.rem(w + d, n_wa), w).start()

    arrived[0, pl.ds(w, 1)] = part[0:1]

    @pl.when(r == 0)
    def _():
        arrived[1] = jnp.zeros_like(arrived[1])

    for d in range(1, n_wa):
        own_copy(lax.rem(w + d, n_wa), lax.rem(w + n_wa - d, n_wa)).wait_recv()

    @pl.when(has_prev)
    def _():
        for d in range(n_wa):
            next_copy(lax.rem(w + d, n_wa), lax.rem(w + n_wa - d, n_wa)).wait_recv()

    halves = []
    for a in range(2):
        blocks = []
        carried = None
        for c in range(n_wa):
            block = arrived[0, c, a] + arrived[1, c, a]
            if carried is not None:
                block = jnp.concatenate([block[0:1] + carried, block[1:]], 0)
            carried = block[pc : pc + 1]
            blocks.append(block[0:pc])
        halves.append(jnp.concatenate(blocks, 0))
    gathered[pl.ds(r, 1)] = jnp.concatenate(halves, 0).astype(BF16)[None]

    def row_copy(target, slot):
        return pltpu.make_async_remote_copy(
            src_ref=gathered.at[slot],
            dst_ref=gathered.at[slot],
            send_sem=row_send.at[target],
            recv_sem=row_recv.at[slot],
            device_id=(target, w),
            device_id_type=MESH,
        )

    @pl.loop(1, n_ha)
    def _(d):
        row_copy(lax.rem(r + d, n_ha), r).start()

    for d in range(1, n_wa):
        own_copy(lax.rem(w + d, n_wa), w).wait_send()

    @pl.when(has_next)
    def _():
        for d in range(n_wa):
            next_copy(lax.rem(w + d, n_wa), w).wait_send()

    @pl.loop(1, n_ha)
    def _(d):
        source = lax.rem(r + n_ha - d, n_ha)
        row_copy(source, source).wait_recv()

    @pl.loop(1, n_ha)
    def _(d):
        row_copy(lax.rem(r + d, n_ha), r).wait_send()


def gather_pooled(n_ha, n_wa, key_tokens, value_tokens, key_kernel, value_kernel):
    own_cols, width = key_tokens.shape[1:]
    pc = own_cols // STRIDE
    span = round_up(pc + 1, 8)
    dma = pltpu.SemaphoreType.DMA
    return pl.pallas_call(
        functools.partial(gather_kernel, n_ha, n_wa, pc),
        out_shape=jax.ShapeDtypeStruct((n_ha, 2 * pc * n_wa, width), BF16),
        in_specs=[pl.BlockSpec(memory_space=pl.ANY)] * 2
        + [pl.BlockSpec(memory_space=pltpu.VMEM)] * 2,
        out_specs=pl.BlockSpec(memory_space=pltpu.VMEM),
        scratch_shapes=[
            pltpu.VMEM((2, 3, own_cols, width), BF16),
            pltpu.VMEM((2, 2, span, width), F32),
            pltpu.VMEM((2, n_wa, 2, span, width), F32),
            dma((4,)),
            dma((n_wa,)),
            dma((n_wa,)),
            dma((n_wa,)),
            dma((n_wa,)),
            dma((n_ha,)),
            dma((n_ha,)),
        ],
        compiler_params=pltpu.CompilerParams(
            collective_id=0, has_side_effects=True, vmem_limit_bytes=32 * 2**20
        ),
        name="pool_gather",
    )(key_tokens, value_tokens, key_kernel, value_kernel)


def window(head):
    low = head * HD // 128 * 128
    high = round_up((head + 1) * HD, 128)
    return low, high


def nt(left, right):
    return lax.dot_general(left, right, (((1,), (1,)), ((), ())), preferred_element_type=F32)


def nn(left, right):
    return lax.dot_general(left, right, (((1,), (0,)), ((), ())), preferred_element_type=F32)


def tn(left, right):
    return lax.dot_general(left, right, (((0,), (0,)), ((), ())), preferred_element_type=F32)


def attention_kernel(
    n_ha, n_wa, pc, own_cols, tile_rows, rows_h,
    queries, out_grad, gathered, height_rows, width_rows,
    query_grad, sums, tables,
    key_win, value_win, height_win, width_win, main_acc, height_acc, value_acc,
    key_full, value_full, height_full, width_full, fold,
):
    kc = pc * n_wa
    kr = n_ha
    keys = kr * kc
    blocks = pc + kc - 1
    scale = HD ** (-0.5)
    tile = tile_rows * own_cols
    tiles = queries.shape[0] // tile
    hrows = tile_rows * kr

    lane = lax.broadcasted_iota(jnp.int32, (1, tile), 1)
    lane_row = lane // own_cols
    lane_col = lane % own_cols
    lane_block = lane_col // STRIDE
    lane_in = lane_col % STRIDE
    in_block = lax.broadcasted_iota(jnp.int32, (1, STRIDE, tile), 1) == lane_in[None]

    for head in range(HEADS):
        low, high = window(head)
        size = high - low
        channel = lax.broadcasted_iota(jnp.int32, (1, size), 1) + low
        mine = (channel >= head * HD) & (channel < (head + 1) * HD)
        zero = jnp.zeros((), BF16)

        pooled = gathered[:, :, low:high].astype(F32)
        pooled = jnp.where(mine[None], pooled, 0.0)
        key_win[:, :size] = pooled[:, :kc].reshape(keys, size).astype(BF16)
        value_win[:, :size] = pooled[:, kc:].reshape(keys, size).astype(BF16)
        height_win[:, :size] = jnp.where(mine, height_rows[:, low:high].astype(F32), 0.0).astype(
            BF16
        )
        width_win[:, :size] = jnp.where(mine, width_rows[:, low:high].astype(F32), 0.0).astype(BF16)

        def step(i, first):
            base = pl.multiple_of(i * tile, tile)
            hbase = pl.multiple_of(i * hrows, hrows)
            q = queries[pl.ds(base, tile), low:high]
            g = out_grad[pl.ds(base, tile), low:high]
            kw_ = key_win[:, :size]
            vw_ = value_win[:, :size]
            hw_ = height_win[pl.ds(hbase, hrows), :size]
            ww_ = width_win[:, :size]
            raw_h = nt(hw_, q)
            raw_w = nt(ww_, q)
            rel_h = raw_h[0:kr]
            for a in range(1, tile_rows):
                rel_h = jnp.where(lane_row == a, raw_h[a * kr : (a + 1) * kr], rel_h)
            picked = jnp.sum(
                jnp.where(in_block, raw_w.reshape(blocks, STRIDE, tile), 0.0), axis=1
            )
            rel_w = picked[pc - 1 : pc - 1 + kc]
            for u in range(1, pc):
                rel_w = jnp.where(lane_block == u, picked[pc - 1 - u : pc - 1 - u + kc], rel_w)
            scores = nt(kw_, q).reshape(kr, kc, tile) * scale + (rel_h[:, None, :] + rel_w[None])
            top = jnp.max(jnp.max(scores, axis=0), axis=0, keepdims=True)
            weights = jnp.exp(scores - top[None])
            total = jnp.sum(jnp.sum(weights, axis=0), axis=0, keepdims=True)
            probs = weights * (1.0 / total)[None]
            probs_low = probs.astype(BF16)
            grad_probs = nt(vw_, g).reshape(kr, kc, tile)
            delta = jnp.sum(
                jnp.sum(probs_low.astype(F32) * grad_probs, axis=0), axis=0, keepdims=True
            )
            grad_scores = probs * (grad_probs - delta[None])
            grad_low = grad_scores.astype(BF16).reshape(keys, tile)
            probs_low = probs_low.reshape(keys, tile)
            grad_h = jnp.sum(grad_scores, axis=1)
            grad_w = jnp.sum(grad_scores, axis=0)
            spread_h = jnp.concatenate(
                [jnp.where(lane_row == a, grad_h, 0.0) for a in range(tile_rows)], 0
            ).astype(BF16)
            shifted = None
            for u in range(pc):
                pieces = []
                if pc - 1 - u:
                    pieces.append(jnp.zeros((pc - 1 - u, tile), F32))
                pieces.append(jnp.where(lane_block == u, grad_w, 0.0))
                if u:
                    pieces.append(jnp.zeros((u, tile), F32))
                piece = jnp.concatenate(pieces, 0)
                shifted = piece if shifted is None else shifted + piece
            spread_w = (
                jnp.where(in_block, shifted[:, None, :], 0.0)
                .reshape(blocks * STRIDE, tile)
                .astype(BF16)
            )
            d_query = tn(grad_low, kw_) * scale + tn(
                jnp.concatenate([spread_h, spread_w], 0), jnp.concatenate([hw_, ww_], 0)
            )
            old = query_grad[pl.ds(base, tile), low:high]
            query_grad[pl.ds(base, tile), low:high] = jnp.where(
                mine, d_query, old.astype(F32)
            ).astype(BF16)
            by_query = nn(jnp.concatenate([grad_low, spread_w, spread_h], 0), q)
            by_grad = nn(probs_low, g)
            split = keys + blocks * STRIDE
            if first:
                main_acc[:, :size] = by_query[:split]
                value_acc[:, :size] = by_grad
            else:
                main_acc[:, :size] += by_query[:split]
                value_acc[:, :size] += by_grad
            height_acc[pl.ds(hbase, hrows), :size] = by_query[split:]

        if head == 0:
            query_grad[...] = jnp.zeros_like(query_grad)
        step(0, True)
        if tiles > 1:

            @pl.loop(1, tiles)
            def _(i):
                step(i, False)

        def merge(full, value):
            if head == 0:
                full[:, low:high] = value
            else:
                full[:, low:high] = jnp.where(mine, value, full[:, low:high])

        merge(key_full, main_acc[:keys, :size] * scale)
        merge(value_full, value_acc[:, :size])
        merge(width_full, main_acc[keys:, :size])
        merge(height_full, height_acc[:, :size])

    width = queries.shape[1]
    sums[...] = jnp.concatenate(
        [key_full[...].reshape(kr, kc, width), value_full[...].reshape(kr, kc, width)], 1
    ).astype(BF16)

    def folded(full):
        value = full[:, 0:HD]
        for head in range(1, HEADS):
            value = value + full[:, head * HD : (head + 1) * HD]
        return value

    tables[...] = jnp.zeros_like(tables)
    r = lax.axis_index("ha")
    w = lax.axis_index("wa")
    fold[...] = folded(height_full)
    per_h = rows_h // STRIDE
    for kh in range(kr):
        at = r + (kr - 1 - kh)
        tables[at // per_h, pl.ds(pl.multiple_of((at % per_h) * STRIDE, STRIDE), STRIDE)] = fold[
            pl.ds(kh, STRIDE, stride=kr)
        ].astype(BF16)
    by_width = folded(width_full)
    per_w = (tables.shape[1] - rows_h) // STRIDE
    for v in range(blocks):
        at = w * pc + (blocks - 1 - v)
        tables[
            at // per_w, pl.ds(pl.multiple_of(rows_h + (at % per_w) * STRIDE, STRIDE), STRIDE)
        ] = by_width[v * STRIDE : (v + 1) * STRIDE].astype(BF16)


def attention(n_ha, n_wa, rows_h, rows_w, queries, out_grad, gathered, height_rows, width_rows):
    own_rows, own_cols, width = queries.shape
    pc = own_cols // STRIDE
    kc = pc * n_wa
    keys = n_ha * kc
    blocks = pc + kc - 1
    tile_rows = max(1, min(own_rows, 256 // own_cols))
    tokens = own_rows * own_cols
    wide = max(window(head)[1] - window(head)[0] for head in range(HEADS))
    vmem = pl.BlockSpec(memory_space=pltpu.VMEM)
    return pl.pallas_call(
        functools.partial(attention_kernel, n_ha, n_wa, pc, own_cols, tile_rows, rows_h),
        out_shape=(
            jax.ShapeDtypeStruct((tokens, width), BF16),
            jax.ShapeDtypeStruct((n_ha, 2 * kc, width), BF16),
            jax.ShapeDtypeStruct((n_ha, rows_h + rows_w, HD), BF16),
        ),
        in_specs=[vmem] * 5,
        out_specs=(vmem,) * 3,
        scratch_shapes=[
            pltpu.VMEM((keys, wide), BF16),
            pltpu.VMEM((keys, wide), BF16),
            pltpu.VMEM((own_rows * n_ha, wide), BF16),
            pltpu.VMEM((blocks * STRIDE, wide), BF16),
            pltpu.VMEM((keys + blocks * STRIDE, wide), F32),
            pltpu.VMEM((own_rows * n_ha, wide), F32),
            pltpu.VMEM((keys, wide), F32),
            pltpu.VMEM((keys, width), F32),
            pltpu.VMEM((keys, width), F32),
            pltpu.VMEM((own_rows * n_ha, width), F32),
            pltpu.VMEM((blocks * STRIDE, width), F32),
            pltpu.VMEM((own_rows * n_ha, HD), F32),
        ],
        compiler_params=pltpu.CompilerParams(vmem_limit_bytes=56 * 2**20),
        name="attention_backward",
    )(queries.reshape(tokens, width), out_grad.reshape(tokens, width), gathered, height_rows, width_rows)


def reduce_kernel(
    n_ha, n_wa, pc,
    sums, tables, cotangent, tables_all,
    sums_in, tables_in, partial, partial_in, slice_out, slice_in,
    sums_send, sums_recv, tables_send, tables_recv,
    own_send, own_recv, below_send, below_recv, slice_send, slice_recv, all_send, all_recv,
):
    r = lax.axis_index("ha")
    w = lax.axis_index("wa")
    kc = pc * n_wa
    has_next = r + 1 < n_ha
    has_prev = r > 0
    barrier = pltpu.get_barrier_semaphore()

    @pl.loop(1, n_ha)
    def _(d):
        pl.semaphore_signal(
            barrier, 1, device_id=(lax.rem(r + d, n_ha), w), device_id_type=MESH
        )

    for d in range(1, n_wa):
        other = lax.rem(w + d, n_wa)
        pl.semaphore_signal(barrier, 1, device_id=(r, other), device_id_type=MESH)

        @pl.when(has_next)
        def _():
            pl.semaphore_signal(barrier, 1, device_id=(r + 1, other), device_id_type=MESH)

        @pl.when(has_prev)
        def _():
            pl.semaphore_signal(barrier, 1, device_id=(r - 1, other), device_id_type=MESH)

    extra = jnp.where(has_next, n_wa - 1, 0) + jnp.where(has_prev, n_wa - 1, 0)
    pl.semaphore_wait(barrier, n_ha - 1 + n_wa - 1 + extra)

    def remote(source, target, send, recv, device):
        return pltpu.make_async_remote_copy(
            src_ref=source, dst_ref=target, send_sem=send, recv_sem=recv,
            device_id=device, device_id_type=MESH,
        )

    def sums_copy(target, slot):
        return remote(
            sums.at[target], sums_in.at[slot], sums_send.at[target], sums_recv.at[slot], (target, w)
        )

    def tables_copy(target, slot):
        return remote(
            tables.at[target], tables_in.at[slot], tables_send.at[target], tables_recv.at[slot],
            (target, w),
        )

    @pl.loop(1, n_ha)
    def _(d):
        target = lax.rem(r + d, n_ha)
        sums_copy(target, r).start()
        tables_copy(target, r).start()

    sums_in[pl.ds(r, 1)] = sums[pl.ds(r, 1)]
    tables_in[pl.ds(r, 1)] = tables[pl.ds(r, 1)]

    @pl.loop(1, n_ha)
    def _(d):
        source = lax.rem(r + n_ha - d, n_ha)
        sums_copy(source, source).wait_recv()
        tables_copy(source, source).wait_recv()

    partial[...] = jnp.sum(sums_in[...].astype(F32), axis=0)
    slice_out[...] = jnp.sum(tables_in[...].astype(F32), axis=0)

    def own_copy(target, slot):
        return remote(
            partial, partial_in.at[0, slot], own_send.at[target], own_recv.at[slot], (r, target)
        )

    def below_copy(target, slot):
        return remote(
            partial, partial_in.at[1, slot], below_send.at[target], below_recv.at[slot],
            (r - 1, target),
        )

    def slice_copy(target, slot):
        return remote(
            slice_out, slice_in.at[slot], slice_send.at[target], slice_recv.at[slot], (r, target)
        )

    for d in range(1, n_wa):
        target = lax.rem(w + d, n_wa)
        slice_copy(target, w).start()
        own_copy(target, w).start()

    @pl.when(has_prev)
    def _():
        for d in range(n_wa):
            below_copy(lax.rem(w + d, n_wa), w).start()

    slice_in[pl.ds(w, 1)] = slice_out[...][None]
    partial_in[0, pl.ds(w, 1)] = partial[...][None]

    for d in range(1, n_wa):
        slice_copy(lax.rem(w + d, n_wa), lax.rem(w + n_wa - d, n_wa)).wait_recv()
    tables_all[pl.ds(r, 1)] = jnp.sum(slice_in[...], axis=0)[None].astype(BF16)

    def all_copy(target, slot):
        return remote(
            tables_all.at[slot], tables_all.at[slot], all_send.at[target], all_recv.at[slot],
            (target, w),
        )

    @pl.loop(1, n_ha)
    def _(d):
        all_copy(lax.rem(r + d, n_ha), r).start()

    @pl.when(jnp.logical_not(has_next))
    def _():
        partial_in[1] = jnp.zeros_like(partial_in[1])

    for d in range(1, n_wa):
        own_copy(lax.rem(w + d, n_wa), lax.rem(w + n_wa - d, n_wa)).wait_recv()

    @pl.when(has_next)
    def _():
        for d in range(n_wa):
            below_copy(lax.rem(w + d, n_wa), lax.rem(w + n_wa - d, n_wa)).wait_recv()

    width = cotangent.shape[-1]
    span = cotangent.shape[2]
    for side in range(2):
        whole = jnp.sum(partial_in[side], axis=0)
        for a in range(2):
            rows = whole[a * kc : (a + 1) * kc]
            chosen = None
            for c in range(n_wa):
                piece = rows[c * pc : min(kc, (c + 1) * pc + 1)]
                piece = jnp.concatenate(
                    [piece, jnp.zeros((span - piece.shape[0], width), F32)], 0
                )
                chosen = piece if chosen is None else jnp.where(w == c, piece, chosen)
            cotangent[side, a] = chosen

    @pl.loop(1, n_ha)
    def _(d):
        target = lax.rem(r + d, n_ha)
        sums_copy(target, r).wait_send()
        tables_copy(target, r).wait_send()

    for d in range(1, n_wa):
        target = lax.rem(w + d, n_wa)
        slice_copy(target, w).wait_send()
        own_copy(target, w).wait_send()

    @pl.when(has_prev)
    def _():
        for d in range(n_wa):
            below_copy(lax.rem(w + d, n_wa), w).wait_send()

    @pl.loop(1, n_ha)
    def _(d):
        source = lax.rem(r + n_ha - d, n_ha)
        all_copy(source, source).wait_recv()

    @pl.loop(1, n_ha)
    def _(d):
        all_copy(lax.rem(r + d, n_ha), r).wait_send()


def reduce_sums(n_ha, n_wa, pc, sums, tables):
    span = round_up(pc + 1, 8)
    rows, width = sums.shape[1:]
    entries = tables.shape[1]
    dma = pltpu.SemaphoreType.DMA
    vmem = pl.BlockSpec(memory_space=pltpu.VMEM)
    return pl.pallas_call(
        functools.partial(reduce_kernel, n_ha, n_wa, pc),
        out_shape=(
            jax.ShapeDtypeStruct((2, 2, span, width), F32),
            jax.ShapeDtypeStruct(tables.shape, BF16),
        ),
        in_specs=[vmem] * 2,
        out_specs=(vmem,) * 2,
        scratch_shapes=[
            pltpu.VMEM((n_ha, rows, width), BF16),
            pltpu.VMEM((n_ha, entries, HD), BF16),
            pltpu.VMEM((rows, width), F32),
            pltpu.VMEM((2, n_wa, rows, width), F32),
            pltpu.VMEM((entries, HD), F32),
            pltpu.VMEM((n_wa, entries, HD), F32),
        ]
        + [dma((n_ha,))] * 4
        + [dma((n_wa,))] * 6
        + [dma((n_ha,))] * 2,
        compiler_params=pltpu.CompilerParams(
            collective_id=1, has_side_effects=True, vmem_limit_bytes=32 * 2**20
        ),
        name="reduce_sums",
    )(sums, tables)


def write_kernel(
    pc, rows_h, cotangent, tables, key_kernel, value_kernel, key_grad, value_grad, height, wide
):
    width = key_grad.shape[-1]
    at = lax.broadcasted_iota(jnp.int32, (STRIDE, 1), 0)
    for a, (kernel, out) in enumerate(((key_kernel, key_grad), (value_kernel, value_grad))):
        out[...] = jnp.zeros_like(out)
        for row, tap, side in ((0, 1, 0), (1, 2, 0), (STRIDE - 1, 0, 1)):
            taps = kernel[tap].astype(F32)
            for k in range(pc):
                here = cotangent[side, a, k : k + 1]
                after = cotangent[side, a, k + 1 : k + 2]
                block = jnp.where(
                    at == 0,
                    here * taps[1:2],
                    jnp.where(
                        at == 1,
                        here * taps[2:3],
                        jnp.where(at == STRIDE - 1, after * taps[0:1], jnp.zeros((STRIDE, width), F32)),
                    ),
                )
                out[row, STRIDE * k : STRIDE * (k + 1)] = block.astype(BF16)
    n_ha = tables.shape[0]
    rows_w = tables.shape[1] - rows_h
    for out, first, size in ((height, 0, rows_h), (wide, rows_h, rows_w)):
        total = out.shape[0]
        for h in range(n_ha):
            count = min(size, total - h * size)
            if count > 0:
                value = tables[h, first : first + size].astype(F32)
                out[h * size : h * size + count] = value[:count]


def write_back(rows_h, cotangent, tables, key_kernel, value_kernel, shape, heights, widths):
    vmem = pl.BlockSpec(memory_space=pltpu.VMEM)
    return pl.pallas_call(
        functools.partial(write_kernel, shape[1] // STRIDE, rows_h),
        out_shape=(
            jax.ShapeDtypeStruct(shape, BF16),
            jax.ShapeDtypeStruct(shape, BF16),
            jax.ShapeDtypeStruct((heights, HD), F32),
            jax.ShapeDtypeStruct((widths, HD), F32),
        ),
        in_specs=[vmem] * 4,
        out_specs=(vmem,) * 4,
        compiler_params=pltpu.CompilerParams(vmem_limit_bytes=32 * 2**20),
        name="write_back",
    )(cotangent, tables, key_kernel, value_kernel)


def on_device(
    queries, key_tokens, value_tokens, out_grad, key_kernel, value_kernel, height_table, width_table
):
    own_rows, own_cols, width = queries.shape
    n_ha = lax.axis_size("ha")
    n_wa = lax.axis_size("wa")
    assert own_rows == STRIDE and own_cols % STRIDE == 0
    pc = own_cols // STRIDE
    kc = pc * n_wa
    blocks = pc + kc - 1
    heights = height_table.shape[0]
    widths = width_table.shape[0]
    rows_h = round_up(-(-heights // n_ha), STRIDE)
    rows_w = round_up(-(-widths // n_ha), STRIDE)
    r = lax.axis_index("ha")
    w = lax.axis_index("wa")
    height_rows = lax.dynamic_slice_in_dim(height_table, r * own_rows, own_rows * n_ha, 0)
    height_rows = height_rows.reshape(n_ha, own_rows, HD)[::-1].transpose(1, 0, 2)
    height_rows = jnp.tile(height_rows.reshape(own_rows * n_ha, HD), (1, HEADS))
    width_rows = lax.dynamic_slice_in_dim(width_table, w * own_cols, blocks * STRIDE, 0)
    width_rows = width_rows.reshape(blocks, STRIDE, HD)[::-1].reshape(blocks * STRIDE, HD)
    width_rows = jnp.tile(width_rows, (1, HEADS))
    gathered = gather_pooled(n_ha, n_wa, key_tokens, value_tokens, key_kernel, value_kernel)
    query_grad, sums, tables = attention(
        n_ha, n_wa, rows_h, rows_w, queries, out_grad, gathered, height_rows, width_rows
    )
    cotangent, tables_all = reduce_sums(n_ha, n_wa, pc, sums, tables)
    key_grad, value_grad, height_grad, width_grad = write_back(
        rows_h, cotangent, tables_all, key_kernel, value_kernel, queries.shape, heights, widths
    )
    return (query_grad.reshape(queries.shape), key_grad, value_grad, height_grad, width_grad)


def solution(mesh):
    placed = (
        P("ha", "wa", None),
        P("ha", "wa", None),
        P("ha", "wa", None),
        P("ha", "wa", None),
        P(),
        P(),
        P(),
        P(),
    )
    return jax.shard_map(
        on_device,
        mesh=mesh,
        in_specs=placed,
        out_specs=(P("ha", "wa", None), P("ha", "wa", None), P("ha", "wa", None), P(), P()),
        check_vma=False,
    )
```

```python
import functools

import jax
import jax.numpy as jnp
from jax import lax
from jax.experimental import pallas as pl
from jax.experimental.pallas import tpu as pltpu
from jax.sharding import PartitionSpec as P

HEADS = 4
HD = 96
KS = 3
STRIDE = 16
MESH = pl.DeviceIdType.MESH
F32 = jnp.float32
BF16 = jnp.bfloat16


def round_up(value, unit):
    return -(-value // unit) * unit


def gather_part(
    n_ha, n_wa, pc,
    key_hbm, value_hbm, key_kernel, value_kernel, gathered,
    tokens, part, arrived, load_sem, own_send, own_recv, next_send, next_recv, row_send, row_recv, prepare,
):
    r = lax.axis_index("ha")
    w = lax.axis_index("wa")
    span = part.shape[2]
    kc = pc * n_wa
    last = tokens.shape[2] // pc
    has_next = r + 1 < n_ha
    has_prev = r > 0

    loads = []
    for a, source in enumerate((key_hbm, value_hbm)):
        loads.append(
            pltpu.make_async_copy(
                source.at[pl.ds(0, 2)], tokens.at[a, pl.ds(0, 2)], load_sem.at[2 * a]
            )
        )
        loads.append(
            pltpu.make_async_copy(
                source.at[pl.ds(STRIDE - 1, 1)], tokens.at[a, pl.ds(2, 1)], load_sem.at[2 * a + 1]
            )
        )
    for load in loads:
        load.start()

    barrier = pltpu.get_barrier_semaphore()

    @pl.loop(1, n_ha)
    def _(d):
        pl.semaphore_signal(
            barrier, 1, device_id=(lax.rem(r + d, n_ha), w), device_id_type=MESH
        )

    for d in range(1, n_wa):
        other = lax.rem(w + d, n_wa)
        pl.semaphore_signal(barrier, 1, device_id=(r, other), device_id_type=MESH)

        @pl.when(has_next)
        def _():
            pl.semaphore_signal(barrier, 1, device_id=(r + 1, other), device_id_type=MESH)

        @pl.when(has_prev)
        def _():
            pl.semaphore_signal(barrier, 1, device_id=(r - 1, other), device_id_type=MESH)

    extra = jnp.where(has_next, n_wa - 1, 0) + jnp.where(has_prev, n_wa - 1, 0)

    for load in loads:
        load.wait()

    def pooled(a, kernel, uses):
        rows = [None] * (pc + 1)

        def add(k, term):
            rows[k] = term if rows[k] is None else rows[k] + term

        for at, tap in uses:
            line = tokens[a, at].astype(F32)
            for k in range(pc):
                for col, to, key in ((0, 1, k), (1, 2, k), (STRIDE - 1, 0, k + 1)):
                    at_col = STRIDE * k + col
                    weight = kernel[tap, to : to + 1].astype(F32)
                    add(key, line[at_col : at_col + 1] * weight)
        return jnp.concatenate(
            rows + [jnp.zeros((span - pc - 1, tokens.shape[-1]), F32)], 0
        )

    for a, kernel in enumerate((key_kernel, value_kernel)):
        part[0, a] = pooled(a, kernel, ((0, 1), (1, 2)))
        part[1, a] = pooled(a, kernel, ((2, 0),))

    pl.semaphore_wait(barrier, n_ha - 1 + n_wa - 1 + extra)

    def own_copy(target, slot):
        return pltpu.make_async_remote_copy(
            src_ref=part.at[0],
            dst_ref=arrived.at[0, slot],
            send_sem=own_send.at[target],
            recv_sem=own_recv.at[slot],
            device_id=(r, target),
            device_id_type=MESH,
        )

    def next_copy(target, slot):
        return pltpu.make_async_remote_copy(
            src_ref=part.at[1],
            dst_ref=arrived.at[1, slot],
            send_sem=next_send.at[target],
            recv_sem=next_recv.at[slot],
            device_id=(r + 1, target),
            device_id_type=MESH,
        )

    for d in range(1, n_wa):
        own_copy(lax.rem(w + d, n_wa), w).start()

    @pl.when(has_next)
    def _():
        for d in range(n_wa):
            next_copy(lax.rem(w + d, n_wa), w).start()

    arrived[0, pl.ds(w, 1)] = part[0:1]
    prepare()

    @pl.when(r == 0)
    def _():
        arrived[1] = jnp.zeros_like(arrived[1])

    for d in range(1, n_wa):
        own_copy(lax.rem(w + d, n_wa), lax.rem(w + n_wa - d, n_wa)).wait_recv()

    @pl.when(has_prev)
    def _():
        for d in range(n_wa):
            next_copy(lax.rem(w + d, n_wa), lax.rem(w + n_wa - d, n_wa)).wait_recv()

    halves = []
    for a in range(2):
        blocks = []
        carried = None
        for c in range(n_wa):
            block = arrived[0, c, a] + arrived[1, c, a]
            if carried is not None:
                block = jnp.concatenate([block[0:1] + carried, block[1:]], 0)
            carried = block[pc : pc + 1]
            blocks.append(block[0:pc])
        halves.append(jnp.concatenate(blocks, 0))
    gathered[pl.ds(r, 1)] = jnp.concatenate(halves, 0).astype(BF16)[None]

    def row_copy(target, slot):
        return pltpu.make_async_remote_copy(
            src_ref=gathered.at[slot],
            dst_ref=gathered.at[slot],
            send_sem=row_send.at[target],
            recv_sem=row_recv.at[slot],
            device_id=(target, w),
            device_id_type=MESH,
        )

    @pl.loop(1, n_ha)
    def _(d):
        row_copy(lax.rem(r + d, n_ha), r).start()

    for d in range(1, n_wa):
        own_copy(lax.rem(w + d, n_wa), w).wait_send()

    @pl.when(has_next)
    def _():
        for d in range(n_wa):
            next_copy(lax.rem(w + d, n_wa), w).wait_send()

    @pl.loop(1, n_ha)
    def _(d):
        source = lax.rem(r + n_ha - d, n_ha)
        row_copy(source, source).wait_recv()

    @pl.loop(1, n_ha)
    def _(d):
        row_copy(lax.rem(r + d, n_ha), r).wait_send()


def window(head):
    low = head * HD // 128 * 128
    high = round_up((head + 1) * HD, 128)
    return low, high


def nt(left, right):
    return lax.dot_general(left, right, (((1,), (1,)), ((), ())), preferred_element_type=F32)


def nn(left, right):
    return lax.dot_general(left, right, (((1,), (0,)), ((), ())), preferred_element_type=F32)


def tn(left, right):
    return lax.dot_general(left, right, (((0,), (0,)), ((), ())), preferred_element_type=F32)


def attention_part(
    n_ha, n_wa, pc, own_cols, tile_rows, rows_h,
    queries, out_grad, gathered, height_rows, width_rows,
    query_grad, sums, tables_h, tables_w, send_lanes,
    key_win, value_win, height_win, width_win, main_acc, height_acc, value_acc,
    key_full, value_full, height_full, width_full, fold,
):
    kc = pc * n_wa
    kr = n_ha
    keys = kr * kc
    blocks = pc + kc - 1
    scale = HD ** (-0.5)
    tile = tile_rows * own_cols
    tiles = queries.shape[0] // tile
    hrows = tile_rows * kr

    lane = lax.broadcasted_iota(jnp.int32, (1, tile), 1)
    lane_row = lane // own_cols
    lane_col = lane % own_cols
    lane_block = lane_col // STRIDE
    lane_in = lane_col % STRIDE
    in_block = lax.broadcasted_iota(jnp.int32, (1, STRIDE, tile), 1) == lane_in[None]

    for head in range(HEADS):
        low, high = window(head)
        size = high - low
        channel = lax.broadcasted_iota(jnp.int32, (1, size), 1) + low
        mine = (channel >= head * HD) & (channel < (head + 1) * HD)
        zero = jnp.zeros((), BF16)

        pooled = gathered[:, :, low:high].astype(F32)
        pooled = jnp.where(mine[None], pooled, 0.0)
        key_win[:, :size] = pooled[:, :kc].reshape(keys, size).astype(BF16)
        value_win[:, :size] = pooled[:, kc:].reshape(keys, size).astype(BF16)
        height_win[:, :size] = jnp.where(mine, height_rows[:, low:high].astype(F32), 0.0).astype(
            BF16
        )
        width_win[:, :size] = jnp.where(mine, width_rows[:, low:high].astype(F32), 0.0).astype(BF16)

        def step(i, first):
            base = pl.multiple_of(i * tile, tile)
            hbase = pl.multiple_of(i * hrows, hrows)
            q = queries[pl.ds(base, tile), low:high]
            g = out_grad[pl.ds(base, tile), low:high]
            kw_ = key_win[:, :size]
            vw_ = value_win[:, :size]
            hw_ = height_win[pl.ds(hbase, hrows), :size]
            ww_ = width_win[:, :size]
            raw_h = nt(hw_, q)
            raw_w = nt(ww_, q)
            rel_h = raw_h[0:kr]
            for a in range(1, tile_rows):
                rel_h = jnp.where(lane_row == a, raw_h[a * kr : (a + 1) * kr], rel_h)
            picked = jnp.sum(
                jnp.where(in_block, raw_w.reshape(blocks, STRIDE, tile), 0.0), axis=1
            )
            rel_w = picked[pc - 1 : pc - 1 + kc]
            for u in range(1, pc):
                rel_w = jnp.where(lane_block == u, picked[pc - 1 - u : pc - 1 - u + kc], rel_w)
            scores = nt(kw_, q).reshape(kr, kc, tile) * scale + (rel_h[:, None, :] + rel_w[None])
            top = jnp.max(jnp.max(scores, axis=0), axis=0, keepdims=True)
            weights = jnp.exp(scores - top[None])
            total = jnp.sum(jnp.sum(weights, axis=0), axis=0, keepdims=True)
            probs = weights * (1.0 / total)[None]
            probs_low = probs.astype(BF16)
            grad_probs = nt(vw_, g).reshape(kr, kc, tile)
            delta = jnp.sum(
                jnp.sum(probs_low.astype(F32) * grad_probs, axis=0), axis=0, keepdims=True
            )
            grad_scores = probs * (grad_probs - delta[None])
            grad_low = grad_scores.astype(BF16).reshape(keys, tile)
            probs_low = probs_low.reshape(keys, tile)
            grad_h = jnp.sum(grad_scores, axis=1)
            grad_w = jnp.sum(grad_scores, axis=0)
            spread_h = jnp.concatenate(
                [jnp.where(lane_row == a, grad_h, 0.0) for a in range(tile_rows)], 0
            ).astype(BF16)
            shifted = None
            for u in range(pc):
                pieces = []
                if pc - 1 - u:
                    pieces.append(jnp.zeros((pc - 1 - u, tile), F32))
                pieces.append(jnp.where(lane_block == u, grad_w, 0.0))
                if u:
                    pieces.append(jnp.zeros((u, tile), F32))
                piece = jnp.concatenate(pieces, 0)
                shifted = piece if shifted is None else shifted + piece
            spread_w = (
                jnp.where(in_block, shifted[:, None, :], 0.0)
                .reshape(blocks * STRIDE, tile)
                .astype(BF16)
            )
            d_query = tn(grad_low, kw_) * scale + tn(
                jnp.concatenate([spread_h, spread_w], 0), jnp.concatenate([hw_, ww_], 0)
            )
            old = query_grad[pl.ds(base, tile), low:high]
            query_grad[pl.ds(base, tile), low:high] = jnp.where(
                mine, d_query, old.astype(F32)
            ).astype(BF16)
            by_query = nn(jnp.concatenate([grad_low, spread_w, spread_h], 0), q)
            by_grad = nn(probs_low, g)
            split = keys + blocks * STRIDE
            if first:
                main_acc[:, :size] = by_query[:split]
                value_acc[:, :size] = by_grad
            else:
                main_acc[:, :size] += by_query[:split]
                value_acc[:, :size] += by_grad
            height_acc[pl.ds(hbase, hrows), :size] = by_query[split:]

        if head == 0:
            query_grad[...] = jnp.zeros_like(query_grad)
        step(0, True)
        if tiles > 1:

            @pl.loop(1, tiles)
            def _(i):
                step(i, False)

        def merge(full, value):
            if head == 0:
                full[:, low:high] = value
            else:
                full[:, low:high] = jnp.where(mine, value, full[:, low:high])

        merge(key_full, main_acc[:keys, :size] * scale)
        merge(value_full, value_acc[:, :size])
        merge(width_full, main_acc[keys:, :size])
        merge(height_full, height_acc[:, :size])
        for t in range(queries.shape[1] // 128):
            if head == -(-128 * (t + 1) // HD) - 1:
                lanes = slice(128 * t, 128 * (t + 1))
                sums[t] = jnp.concatenate(
                    [
                        key_full[:, lanes].reshape(kr, kc, 128),
                        value_full[:, lanes].reshape(kr, kc, 128),
                    ],
                    1,
                ).astype(BF16)
                send_lanes(t)

    def folded(full):
        value = full[:, 0:HD]
        for head in range(1, HEADS):
            value = value + full[:, head * HD : (head + 1) * HD]
        return value

    tables_h[...] = jnp.zeros_like(tables_h)
    tables_w[...] = jnp.zeros_like(tables_w)
    r = lax.axis_index("ha")
    w = lax.axis_index("wa")
    fold[...] = folded(height_full)
    per_h = rows_h // STRIDE
    for kh in range(kr):
        at = r + (kr - 1 - kh)
        tables_h[at // per_h, pl.ds(pl.multiple_of((at % per_h) * STRIDE, STRIDE), STRIDE)] = fold[
            pl.ds(kh, STRIDE, stride=kr)
        ].astype(BF16)
    by_width = folded(width_full)
    per_w = tables_w.shape[1] // STRIDE
    for v in range(blocks):
        at = w * pc + (blocks - 1 - v)
        tables_w[at // per_w, pl.ds(pl.multiple_of((at % per_w) * STRIDE, STRIDE), STRIDE)] = (
            by_width[v * STRIDE : (v + 1) * STRIDE].astype(BF16)
        )


def remote(source, target, send, recv, device):
    return pltpu.make_async_remote_copy(
        src_ref=source, dst_ref=target, send_sem=send, recv_sem=recv,
        device_id=device, device_id_type=MESH,
    )


def reduce_part(
    n_ha, n_wa, pc, sums_copy,
    sums, tables_h, tables_w, cotangent, tables_all,
    sums_in, tables_h_in, tables_w_in, partial, partial_in, slice_out, slice_in,
    h_send, h_recv, w_send, w_recv,
    own_send, own_recv, below_send, below_recv, slice_send, slice_recv, all_send, all_recv,
):
    r = lax.axis_index("ha")
    w = lax.axis_index("wa")
    kc = pc * n_wa
    has_next = r + 1 < n_ha
    has_prev = r > 0
    lanes = sums.shape[0]
    rows_h = tables_h.shape[1]
    rows_w = tables_w.shape[1]
    per_h = rows_h // STRIDE
    per_w = rows_w // STRIDE
    blocks = pc + kc - 1

    def meets_h(source, owner):
        return (per_h * owner + per_h > source) & (per_h * owner < source + n_ha)

    def meets_w(owner):
        return (per_w * owner + per_w > pc * w) & (per_w * owner < pc * w + blocks)

    def h_copy(target, slot):
        return remote(
            tables_h.at[target], tables_h_in.at[slot], h_send.at[target], h_recv.at[slot],
            (target, w),
        )

    def w_copy(target, slot):
        return remote(
            tables_w.at[target], tables_w_in.at[slot], w_send.at[target], w_recv.at[slot],
            (target, w),
        )

    @pl.loop(1, n_ha)
    def _(d):
        target = lax.rem(r + d, n_ha)

        @pl.when(meets_h(r, target))
        def _():
            h_copy(target, r).start()

        @pl.when(meets_w(target))
        def _():
            w_copy(target, r).start()

    for t in range(lanes):
        sums_in[t, pl.ds(r, 1)] = sums[t, pl.ds(r, 1)]
    tables_h_in[pl.ds(r, 1)] = tables_h[pl.ds(r, 1)]
    tables_w_in[pl.ds(r, 1)] = tables_w[pl.ds(r, 1)]

    @pl.loop(1, n_ha)
    def _(d):
        source = lax.rem(r + n_ha - d, n_ha)
        for t in range(lanes):
            sums_copy(t, source, source).wait_recv()

    for t in range(lanes):
        partial[:, 128 * t : 128 * (t + 1)] = jnp.sum(sums_in[t].astype(F32), axis=0)

    def own_copy(target, slot):
        return remote(
            partial, partial_in.at[0, slot], own_send.at[target], own_recv.at[slot], (r, target)
        )

    def below_copy(target, slot):
        return remote(
            partial, partial_in.at[1, slot], below_send.at[target], below_recv.at[slot],
            (r - 1, target),
        )

    def slice_copy(target, slot):
        return remote(
            slice_out, slice_in.at[slot], slice_send.at[target], slice_recv.at[slot], (r, target)
        )

    for d in range(1, n_wa):
        own_copy(lax.rem(w + d, n_wa), w).start()

    @pl.when(has_prev)
    def _():
        for d in range(n_wa):
            below_copy(lax.rem(w + d, n_wa), w).start()

    @pl.loop(1, n_ha)
    def _(d):
        source = lax.rem(r + n_ha - d, n_ha)

        @pl.when(meets_h(source, r))
        def _():
            h_copy(source, source).wait_recv()

        @pl.when(meets_w(r))
        def _():
            w_copy(source, source).wait_recv()

    slice_out[0:rows_h] = jnp.sum(tables_h_in[...].astype(F32), axis=0)
    slice_out[rows_h:] = jnp.sum(tables_w_in[...].astype(F32), axis=0)

    for d in range(1, n_wa):
        slice_copy(lax.rem(w + d, n_wa), w).start()

    slice_in[pl.ds(w, 1)] = slice_out[...][None]
    partial_in[0, pl.ds(w, 1)] = partial[...][None]

    for d in range(1, n_wa):
        slice_copy(lax.rem(w + d, n_wa), lax.rem(w + n_wa - d, n_wa)).wait_recv()
    tables_all[pl.ds(r, 1)] = jnp.sum(slice_in[...], axis=0)[None].astype(BF16)

    def all_copy(target, slot):
        return remote(
            tables_all.at[slot], tables_all.at[slot], all_send.at[target], all_recv.at[slot],
            (target, w),
        )

    @pl.loop(1, n_ha)
    def _(d):
        all_copy(lax.rem(r + d, n_ha), r).start()

    @pl.when(jnp.logical_not(has_next))
    def _():
        partial_in[1] = jnp.zeros_like(partial_in[1])

    for d in range(1, n_wa):
        own_copy(lax.rem(w + d, n_wa), lax.rem(w + n_wa - d, n_wa)).wait_recv()

    @pl.when(has_next)
    def _():
        for d in range(n_wa):
            below_copy(lax.rem(w + d, n_wa), lax.rem(w + n_wa - d, n_wa)).wait_recv()

    width = cotangent.shape[-1]
    span = cotangent.shape[2]
    for side in range(2):
        whole = jnp.sum(partial_in[side], axis=0)
        for a in range(2):
            rows = whole[a * kc : (a + 1) * kc]
            chosen = None
            for c in range(n_wa):
                piece = rows[c * pc : min(kc, (c + 1) * pc + 1)]
                piece = jnp.concatenate(
                    [piece, jnp.zeros((span - piece.shape[0], width), F32)], 0
                )
                chosen = piece if chosen is None else jnp.where(w == c, piece, chosen)
            cotangent[side, a] = chosen

    @pl.loop(1, n_ha)
    def _(d):
        target = lax.rem(r + d, n_ha)
        for t in range(lanes):
            sums_copy(t, target, r).wait_send()

        @pl.when(meets_h(r, target))
        def _():
            h_copy(target, r).wait_send()

        @pl.when(meets_w(target))
        def _():
            w_copy(target, r).wait_send()

    for d in range(1, n_wa):
        target = lax.rem(w + d, n_wa)
        slice_copy(target, w).wait_send()
        own_copy(target, w).wait_send()

    @pl.when(has_prev)
    def _():
        for d in range(n_wa):
            below_copy(lax.rem(w + d, n_wa), w).wait_send()

    @pl.loop(1, n_ha)
    def _(d):
        source = lax.rem(r + n_ha - d, n_ha)
        all_copy(source, source).wait_recv()

    @pl.loop(1, n_ha)
    def _(d):
        all_copy(lax.rem(r + d, n_ha), r).wait_send()


def fused_kernel(
    n_ha, n_wa, pc, own_cols, tile_rows, rows_h,
    key_hbm, value_hbm, query_hbm, grad_hbm, key_kernel, value_kernel, height_table, width_table,
    query_out, cotangent, tables_all,
    queries, out_grad, query_grad, gathered, sums, tables_h, tables_w, sums_in, tables_h_in,
    tables_w_in, height_float, height_rows, width_rows, big_send, sums_send, sums_recv,
    *rest,
):
    gather_refs, attention_refs, reduce_refs = rest[:10], rest[10:22], rest[22:]
    r = lax.axis_index("ha")
    w = lax.axis_index("wa")
    kc = pc * n_wa
    blocks = pc + kc - 1
    fetch = [
        pltpu.make_async_copy(query_hbm, queries, big_send.at[0]),
        pltpu.make_async_copy(grad_hbm, out_grad, big_send.at[1]),
    ]
    tables_h_in[...] = jnp.zeros_like(tables_h_in)
    tables_w_in[...] = jnp.zeros_like(tables_w_in)

    def prepare():
        for copy in fetch:
            copy.start()
        for v in range(n_ha):
            start = pl.multiple_of(r * STRIDE + v * STRIDE, STRIDE)
            height_float[pl.ds(n_ha - 1 - v, STRIDE, stride=n_ha)] = height_table[
                pl.ds(start, STRIDE)
            ].astype(F32)
        once = height_float[...]
        height_rows[...] = jnp.concatenate([once] * HEADS, 1).astype(BF16)
        for v in range(blocks):
            start = pl.multiple_of(w * own_cols + v * STRIDE, STRIDE)
            once = width_table[pl.ds(start, STRIDE)].astype(F32)
            width_rows[(blocks - 1 - v) * STRIDE : (blocks - v) * STRIDE] = jnp.concatenate(
                [once] * HEADS, 1
            ).astype(BF16)

    gather_part(
        n_ha, n_wa, pc, key_hbm, value_hbm, key_kernel, value_kernel, gathered, *gather_refs,
        prepare,
    )
    for copy in fetch:
        copy.wait()

    def sums_copy(t, target, slot):
        return remote(
            sums.at[t, target], sums_in.at[t, slot], sums_send.at[t, target], sums_recv.at[t, slot],
            (target, w),
        )

    def send_lanes(t):
        @pl.loop(1, n_ha)
        def _(d):
            sums_copy(t, lax.rem(r + d, n_ha), r).start()

    attention_part(
        n_ha, n_wa, pc, own_cols, tile_rows, rows_h,
        queries, out_grad, gathered, height_rows, width_rows,
        query_grad, sums, tables_h, tables_w, send_lanes, *attention_refs,
    )
    put = pltpu.make_async_copy(query_grad, query_out, big_send.at[2])
    put.start()
    reduce_part(
        n_ha, n_wa, pc, sums_copy, sums, tables_h, tables_w, cotangent, tables_all,
        sums_in, tables_h_in, tables_w_in, *reduce_refs,
    )
    put.wait()


def fused(
    n_ha, n_wa, rows_h, rows_w,
    queries, key_tokens, value_tokens, out_grad, key_kernel, value_kernel, height_table, width_table,
):
    own_rows, own_cols, width = queries.shape
    pc = own_cols // STRIDE
    kc = pc * n_wa
    keys = n_ha * kc
    blocks = pc + kc - 1
    span = round_up(pc + 1, 8)
    lanes = width // 128
    entries = rows_h + rows_w
    tile_rows = max(1, min(own_rows, 256 // own_cols))
    tokens = own_rows * own_cols
    wide = max(window(head)[1] - window(head)[0] for head in range(HEADS))
    vmem = pl.BlockSpec(memory_space=pltpu.VMEM)
    anywhere = pl.BlockSpec(memory_space=pl.ANY)
    dma = pltpu.SemaphoreType.DMA
    ram = pltpu.VMEM
    return pl.pallas_call(
        functools.partial(fused_kernel, n_ha, n_wa, pc, own_cols, tile_rows, rows_h),
        out_shape=(
            jax.ShapeDtypeStruct((tokens, width), BF16),
            jax.ShapeDtypeStruct((2, 2, span, width), F32),
            jax.ShapeDtypeStruct((n_ha, entries, HD), BF16),
        ),
        in_specs=[anywhere] * 4 + [vmem] * 4,
        out_specs=(anywhere, vmem, vmem),
        scratch_shapes=[
            ram((tokens, width), BF16),
            ram((tokens, width), BF16),
            ram((tokens, width), BF16),
            ram((n_ha, 2 * kc, width), BF16),
            ram((lanes, n_ha, 2 * kc, 128), BF16),
            ram((n_ha, rows_h, HD), BF16),
            ram((n_ha, rows_w, HD), BF16),
            ram((lanes, n_ha, 2 * kc, 128), BF16),
            ram((n_ha, rows_h, HD), BF16),
            ram((n_ha, rows_w, HD), BF16),
            ram((own_rows * n_ha, HD), F32),
            ram((own_rows * n_ha, width), BF16),
            ram((blocks * STRIDE, width), BF16),
            dma((3,)),
            dma((lanes, n_ha)),
            dma((lanes, n_ha)),
            ram((2, 3, own_cols, width), BF16),
            ram((2, 2, span, width), F32),
            ram((2, n_wa, 2, span, width), F32),
            dma((4,)),
            dma((n_wa,)),
            dma((n_wa,)),
            dma((n_wa,)),
            dma((n_wa,)),
            dma((n_ha,)),
            dma((n_ha,)),
            ram((keys, wide), BF16),
            ram((keys, wide), BF16),
            ram((own_rows * n_ha, wide), BF16),
            ram((blocks * STRIDE, wide), BF16),
            ram((keys + blocks * STRIDE, wide), F32),
            ram((own_rows * n_ha, wide), F32),
            ram((keys, wide), F32),
            ram((keys, width), F32),
            ram((keys, width), F32),
            ram((own_rows * n_ha, width), F32),
            ram((blocks * STRIDE, width), F32),
            ram((own_rows * n_ha, HD), F32),
            ram((2 * kc, width), F32),
            ram((2, n_wa, 2 * kc, width), F32),
            ram((entries, HD), F32),
            ram((n_wa, entries, HD), F32),
        ]
        + [dma((n_ha,))] * 4
        + [dma((n_wa,))] * 6
        + [dma((n_ha,))] * 2,
        compiler_params=pltpu.CompilerParams(
            collective_id=0, has_side_effects=True, vmem_limit_bytes=56 * 2**20
        ),
        name="pooled_attention",
    )(
        key_tokens, value_tokens, queries.reshape(tokens, width), out_grad.reshape(tokens, width),
        key_kernel, value_kernel, height_table, width_table,
    )


def write_kernel(
    pc, rows_h, cotangent, tables, key_kernel, value_kernel, key_out, value_out, height, wide,
    middle, edges, done,
):
    width = edges.shape[-1]
    middle[...] = jnp.zeros_like(middle)
    copies = []
    for a, out in enumerate((key_out, value_out)):
        copies.append(
            pltpu.make_async_copy(middle, out.at[pl.ds(2, STRIDE - 3)], done.at[3 * a])
        )
        copies[-1].start()
    edges[...] = jnp.zeros_like(edges)
    at = lax.broadcasted_iota(jnp.int32, (STRIDE, 1), 0)
    for a, (kernel, out) in enumerate(((key_kernel, key_out), (value_kernel, value_out))):
        for row, tap, side in ((0, 1, 0), (1, 2, 0), (2, 0, 1)):
            taps = kernel[tap].astype(F32)
            for k in range(pc):
                here = cotangent[side, a, k : k + 1]
                after = cotangent[side, a, k + 1 : k + 2]
                block = jnp.where(
                    at == 0,
                    here * taps[1:2],
                    jnp.where(
                        at == 1,
                        here * taps[2:3],
                        jnp.where(at == STRIDE - 1, after * taps[0:1], jnp.zeros((STRIDE, width), F32)),
                    ),
                )
                edges[a, row, STRIDE * k : STRIDE * (k + 1)] = block.astype(BF16)
        copies.append(
            pltpu.make_async_copy(edges.at[a, pl.ds(0, 2)], out.at[pl.ds(0, 2)], done.at[3 * a + 1])
        )
        copies[-1].start()
        copies.append(
            pltpu.make_async_copy(
                edges.at[a, pl.ds(2, 1)], out.at[pl.ds(STRIDE - 1, 1)], done.at[3 * a + 2]
            )
        )
        copies[-1].start()
    n_ha = tables.shape[0]
    rows_w = tables.shape[1] - rows_h
    for out, first, size in ((height, 0, rows_h), (wide, rows_h, rows_w)):
        total = out.shape[0]
        for h in range(n_ha):
            count = min(size, total - h * size)
            if count > 0:
                value = tables[h, first : first + size].astype(F32)
                out[h * size : h * size + count] = value[:count]
    for copy in copies:
        copy.wait()


def write_back(rows_h, cotangent, tables, key_kernel, value_kernel, shape, heights, widths):
    vmem = pl.BlockSpec(memory_space=pltpu.VMEM)
    return pl.pallas_call(
        functools.partial(write_kernel, shape[1] // STRIDE, rows_h),
        out_shape=(
            jax.ShapeDtypeStruct(shape, BF16),
            jax.ShapeDtypeStruct(shape, BF16),
            jax.ShapeDtypeStruct((heights, HD), F32),
            jax.ShapeDtypeStruct((widths, HD), F32),
        ),
        in_specs=[vmem] * 4,
        out_specs=(pl.BlockSpec(memory_space=pl.ANY),) * 2 + (vmem,) * 2,
        scratch_shapes=[
            pltpu.VMEM((STRIDE - 3,) + shape[1:], BF16),
            pltpu.VMEM((2, 3) + shape[1:], BF16),
            pltpu.SemaphoreType.DMA((6,)),
        ],
        compiler_params=pltpu.CompilerParams(vmem_limit_bytes=32 * 2**20),
        name="write_back",
    )(cotangent, tables, key_kernel, value_kernel)


def on_device(
    queries, key_tokens, value_tokens, out_grad, key_kernel, value_kernel, height_table, width_table
):
    own_rows, own_cols, width = queries.shape
    n_ha = lax.axis_size("ha")
    n_wa = lax.axis_size("wa")
    assert own_rows == STRIDE and own_cols % STRIDE == 0
    heights = height_table.shape[0]
    widths = width_table.shape[0]
    rows_h = round_up(-(-heights // n_ha), STRIDE)
    rows_w = round_up(-(-widths // n_ha), STRIDE)
    query_grad, cotangent, tables_all = fused(
        n_ha, n_wa, rows_h, rows_w,
        queries, key_tokens, value_tokens, out_grad, key_kernel, value_kernel, height_table,
        width_table,
    )
    key_grad, value_grad, height_grad, width_grad = write_back(
        rows_h, cotangent, tables_all, key_kernel, value_kernel, queries.shape, heights, widths
    )
    return (query_grad.reshape(queries.shape), key_grad, value_grad, height_grad, width_grad)


def solution(mesh):
    placed = (
        P("ha", "wa", None),
        P("ha", "wa", None),
        P("ha", "wa", None),
        P("ha", "wa", None),
        P(),
        P(),
        P(),
        P(),
    )
    return jax.shard_map(
        on_device,
        mesh=mesh,
        in_specs=placed,
        out_specs=(P("ha", "wa", None), P("ha", "wa", None), P("ha", "wa", None), P(), P()),
        check_vma=False,
    )
```

```python
import functools

import jax
import jax.numpy as jnp
from jax import lax
from jax.experimental import pallas as pl
from jax.experimental.pallas import tpu as pltpu
from jax.sharding import PartitionSpec as P

HEADS = 4
HD = 96
KS = 3
STRIDE = 16
MESH = pl.DeviceIdType.MESH
F32 = jnp.float32
BF16 = jnp.bfloat16


def round_up(value, unit):
    return -(-value // unit) * unit


def gather_part(
    n_ha, n_wa, pc,
    key_hbm, value_hbm, key_kernel, value_kernel, gathered,
    tokens, part, arrived, load_sem, own_send, own_recv, next_send, next_recv, row_send, row_recv, prepare,
):
    r = lax.axis_index("ha")
    w = lax.axis_index("wa")
    span = part.shape[2]
    kc = pc * n_wa
    last = tokens.shape[2] // pc
    has_next = r + 1 < n_ha
    has_prev = r > 0

    loads = []
    for a, source in enumerate((key_hbm, value_hbm)):
        loads.append(
            pltpu.make_async_copy(
                source.at[pl.ds(0, 2)], tokens.at[a, pl.ds(0, 2)], load_sem.at[2 * a]
            )
        )
        loads.append(
            pltpu.make_async_copy(
                source.at[pl.ds(STRIDE - 1, 1)], tokens.at[a, pl.ds(2, 1)], load_sem.at[2 * a + 1]
            )
        )
    for load in loads:
        load.start()

    barrier = pltpu.get_barrier_semaphore()

    @pl.loop(1, n_ha)
    def _(d):
        pl.semaphore_signal(
            barrier, 1, device_id=(lax.rem(r + d, n_ha), w), device_id_type=MESH
        )

    for d in range(1, n_wa):
        other = lax.rem(w + d, n_wa)
        pl.semaphore_signal(barrier, 1, device_id=(r, other), device_id_type=MESH)

        @pl.when(has_next)
        def _():
            pl.semaphore_signal(barrier, 1, device_id=(r + 1, other), device_id_type=MESH)

        @pl.when(has_prev)
        def _():
            pl.semaphore_signal(barrier, 1, device_id=(r - 1, other), device_id_type=MESH)

    extra = jnp.where(has_next, n_wa - 1, 0) + jnp.where(has_prev, n_wa - 1, 0)

    for load in loads:
        load.wait()

    def pooled(a, kernel, uses):
        rows = [None] * (pc + 1)

        def add(k, term):
            rows[k] = term if rows[k] is None else rows[k] + term

        for at, tap in uses:
            line = tokens[a, at].astype(F32)
            for k in range(pc):
                for col, to, key in ((0, 1, k), (1, 2, k), (STRIDE - 1, 0, k + 1)):
                    at_col = STRIDE * k + col
                    weight = kernel[tap, to : to + 1].astype(F32)
                    add(key, line[at_col : at_col + 1] * weight)
        return jnp.concatenate(
            rows + [jnp.zeros((span - pc - 1, tokens.shape[-1]), F32)], 0
        )

    for a, kernel in enumerate((key_kernel, value_kernel)):
        part[0, a] = pooled(a, kernel, ((0, 1), (1, 2)))
        part[1, a] = pooled(a, kernel, ((2, 0),))

    pl.semaphore_wait(barrier, n_ha - 1 + n_wa - 1 + extra)

    def own_copy(target, slot):
        return pltpu.make_async_remote_copy(
            src_ref=part.at[0],
            dst_ref=arrived.at[0, slot],
            send_sem=own_send.at[target],
            recv_sem=own_recv.at[slot],
            device_id=(r, target),
            device_id_type=MESH,
        )

    def next_copy(target, slot):
        return pltpu.make_async_remote_copy(
            src_ref=part.at[1],
            dst_ref=arrived.at[1, slot],
            send_sem=next_send.at[target],
            recv_sem=next_recv.at[slot],
            device_id=(r + 1, target),
            device_id_type=MESH,
        )

    for d in range(1, n_wa):
        own_copy(lax.rem(w + d, n_wa), w).start()

    @pl.when(has_next)
    def _():
        for d in range(n_wa):
            next_copy(lax.rem(w + d, n_wa), w).start()

    arrived[0, pl.ds(w, 1)] = part[0:1]
    prepare()

    @pl.when(r == 0)
    def _():
        arrived[1] = jnp.zeros_like(arrived[1])

    for d in range(1, n_wa):
        own_copy(lax.rem(w + d, n_wa), lax.rem(w + n_wa - d, n_wa)).wait_recv()

    @pl.when(has_prev)
    def _():
        for d in range(n_wa):
            next_copy(lax.rem(w + d, n_wa), lax.rem(w + n_wa - d, n_wa)).wait_recv()

    halves = []
    for a in range(2):
        blocks = []
        carried = None
        for c in range(n_wa):
            block = arrived[0, c, a] + arrived[1, c, a]
            if carried is not None:
                block = jnp.concatenate([block[0:1] + carried, block[1:]], 0)
            carried = block[pc : pc + 1]
            blocks.append(block[0:pc])
        halves.append(jnp.concatenate(blocks, 0))
    gathered[pl.ds(r, 1)] = jnp.concatenate(halves, 0).astype(BF16)[None]

    def row_copy(target, slot):
        return pltpu.make_async_remote_copy(
            src_ref=gathered.at[slot],
            dst_ref=gathered.at[slot],
            send_sem=row_send.at[target],
            recv_sem=row_recv.at[slot],
            device_id=(target, w),
            device_id_type=MESH,
        )

    @pl.loop(1, n_ha)
    def _(d):
        row_copy(lax.rem(r + d, n_ha), r).start()

    for d in range(1, n_wa):
        own_copy(lax.rem(w + d, n_wa), w).wait_send()

    @pl.when(has_next)
    def _():
        for d in range(n_wa):
            next_copy(lax.rem(w + d, n_wa), w).wait_send()

    @pl.loop(1, n_ha)
    def _(d):
        source = lax.rem(r + n_ha - d, n_ha)
        row_copy(source, source).wait_recv()

    @pl.loop(1, n_ha)
    def _(d):
        row_copy(lax.rem(r + d, n_ha), r).wait_send()


def window(head):
    low = head * HD // 128 * 128
    high = round_up((head + 1) * HD, 128)
    return low, high


def nt(left, right):
    return lax.dot_general(left, right, (((1,), (1,)), ((), ())), preferred_element_type=F32)


def nn(left, right):
    return lax.dot_general(left, right, (((1,), (0,)), ((), ())), preferred_element_type=F32)


def tn(left, right):
    return lax.dot_general(left, right, (((0,), (0,)), ((), ())), preferred_element_type=F32)


def attention_part(
    n_ha, n_wa, pc, own_cols, tile_rows, rows_h,
    queries, out_grad, gathered, height_rows, width_rows,
    query_grad, sums, tables_h, tables_w, send_lanes,
    key_win, value_win, height_win, width_win, main_acc, height_acc, value_acc,
    key_full, value_full, height_full, width_full, fold,
):
    kc = pc * n_wa
    kr = n_ha
    keys = kr * kc
    blocks = pc + kc - 1
    scale = HD ** (-0.5)
    tile = tile_rows * own_cols
    tiles = queries.shape[0] // tile
    hrows = tile_rows * kr

    lane = lax.broadcasted_iota(jnp.int32, (1, tile), 1)
    lane_row = lane // own_cols
    lane_col = lane % own_cols
    lane_block = lane_col // STRIDE
    lane_in = lane_col % STRIDE
    in_block = lax.broadcasted_iota(jnp.int32, (1, STRIDE, tile), 1) == lane_in[None]

    for head in range(HEADS):
        low, high = window(head)
        size = high - low
        channel = lax.broadcasted_iota(jnp.int32, (1, size), 1) + low
        mine = (channel >= head * HD) & (channel < (head + 1) * HD)
        zero = jnp.zeros((), BF16)

        pooled = gathered[:, :, low:high].astype(F32)
        pooled = jnp.where(mine[None], pooled, 0.0)
        key_win[:, :size] = pooled[:, :kc].reshape(keys, size).astype(BF16)
        value_win[:, :size] = pooled[:, kc:].reshape(keys, size).astype(BF16)
        height_win[:, :size] = jnp.where(mine, height_rows[:, low:high].astype(F32), 0.0).astype(
            BF16
        )
        width_win[:, :size] = jnp.where(mine, width_rows[:, low:high].astype(F32), 0.0).astype(BF16)

        def step(i, first):
            base = pl.multiple_of(i * tile, tile)
            hbase = pl.multiple_of(i * hrows, hrows)
            q = queries[pl.ds(base, tile), low:high]
            g = out_grad[pl.ds(base, tile), low:high]
            kw_ = key_win[:, :size]
            vw_ = value_win[:, :size]
            hw_ = height_win[pl.ds(hbase, hrows), :size]
            ww_ = width_win[:, :size]
            raw = nt(jnp.concatenate([kw_, ww_, hw_], 0), q)
            raw_w = raw[keys : keys + blocks * STRIDE]
            raw_h = raw[keys + blocks * STRIDE :]
            rel_h = raw_h[0:kr]
            for a in range(1, tile_rows):
                rel_h = jnp.where(lane_row == a, raw_h[a * kr : (a + 1) * kr], rel_h)
            picked = jnp.sum(
                jnp.where(in_block, raw_w.reshape(blocks, STRIDE, tile), 0.0), axis=1
            )
            rel_w = picked[pc - 1 : pc - 1 + kc]
            for u in range(1, pc):
                rel_w = jnp.where(lane_block == u, picked[pc - 1 - u : pc - 1 - u + kc], rel_w)
            scores = raw[:keys].reshape(kr, kc, tile) * scale + (rel_h[:, None, :] + rel_w[None])
            top = jnp.max(jnp.max(scores, axis=0), axis=0, keepdims=True)
            weights = jnp.exp(scores - top[None])
            total = jnp.sum(jnp.sum(weights, axis=0), axis=0, keepdims=True)
            probs = weights * (1.0 / total)[None]
            probs_low = probs.astype(BF16)
            grad_probs = nt(vw_, g).reshape(kr, kc, tile)
            delta = jnp.sum(
                jnp.sum(probs_low.astype(F32) * grad_probs, axis=0), axis=0, keepdims=True
            )
            grad_scores = probs * (grad_probs - delta[None])
            grad_low = grad_scores.astype(BF16).reshape(keys, tile)
            probs_low = probs_low.reshape(keys, tile)
            grad_h = jnp.sum(grad_scores, axis=1)
            grad_w = jnp.sum(grad_scores, axis=0)
            spread_h = jnp.concatenate(
                [jnp.where(lane_row == a, grad_h, 0.0) for a in range(tile_rows)], 0
            ).astype(BF16)
            shifted = None
            for u in range(pc):
                pieces = []
                if pc - 1 - u:
                    pieces.append(jnp.zeros((pc - 1 - u, tile), F32))
                pieces.append(jnp.where(lane_block == u, grad_w, 0.0))
                if u:
                    pieces.append(jnp.zeros((u, tile), F32))
                piece = jnp.concatenate(pieces, 0)
                shifted = piece if shifted is None else shifted + piece
            spread_w = (
                jnp.where(in_block, shifted[:, None, :], 0.0)
                .reshape(blocks * STRIDE, tile)
                .astype(BF16)
            )
            d_query = tn(grad_low, kw_) * scale + tn(
                jnp.concatenate([spread_h, spread_w], 0), jnp.concatenate([hw_, ww_], 0)
            )
            old = query_grad[pl.ds(base, tile), low:high]
            query_grad[pl.ds(base, tile), low:high] = jnp.where(
                mine, d_query, old.astype(F32)
            ).astype(BF16)
            by_query = nn(jnp.concatenate([grad_low, spread_w, spread_h], 0), q)
            by_grad = nn(probs_low, g)
            split = keys + blocks * STRIDE
            if first:
                main_acc[:, :size] = by_query[:split]
                value_acc[:, :size] = by_grad
            else:
                main_acc[:, :size] += by_query[:split]
                value_acc[:, :size] += by_grad
            height_acc[pl.ds(hbase, hrows), :size] = by_query[split:]

        if head == 0:
            query_grad[...] = jnp.zeros_like(query_grad)
        step(0, True)
        if tiles > 1:

            @pl.loop(1, tiles, unroll=tiles - 1 if keys <= 256 else 1)
            def _(i):
                step(i, False)

        def merge(full, value):
            if head == 0:
                full[:, low:high] = value
            else:
                full[:, low:high] = jnp.where(mine, value, full[:, low:high])

        merge(key_full, main_acc[:keys, :size] * scale)
        merge(value_full, value_acc[:, :size])
        merge(width_full, main_acc[keys:, :size])
        merge(height_full, height_acc[:, :size])
        for t in range(queries.shape[1] // 128):
            if head == -(-128 * (t + 1) // HD) - 1:
                lanes = slice(128 * t, 128 * (t + 1))
                sums[t] = jnp.concatenate(
                    [
                        key_full[:, lanes].reshape(kr, kc, 128),
                        value_full[:, lanes].reshape(kr, kc, 128),
                    ],
                    1,
                ).astype(BF16)
                send_lanes(t)

    def folded(full):
        value = full[:, 0:HD]
        for head in range(1, HEADS):
            value = value + full[:, head * HD : (head + 1) * HD]
        return value

    tables_h[...] = jnp.zeros_like(tables_h)
    tables_w[...] = jnp.zeros_like(tables_w)
    r = lax.axis_index("ha")
    w = lax.axis_index("wa")
    fold[...] = folded(height_full)
    per_h = rows_h // STRIDE
    for kh in range(kr):
        at = r + (kr - 1 - kh)
        tables_h[at // per_h, pl.ds(pl.multiple_of((at % per_h) * STRIDE, STRIDE), STRIDE)] = fold[
            pl.ds(kh, STRIDE, stride=kr)
        ].astype(BF16)
    by_width = folded(width_full)
    per_w = tables_w.shape[1] // STRIDE
    for v in range(blocks):
        at = w * pc + (blocks - 1 - v)
        tables_w[at // per_w, pl.ds(pl.multiple_of((at % per_w) * STRIDE, STRIDE), STRIDE)] = (
            by_width[v * STRIDE : (v + 1) * STRIDE].astype(BF16)
        )


def remote(source, target, send, recv, device):
    return pltpu.make_async_remote_copy(
        src_ref=source, dst_ref=target, send_sem=send, recv_sem=recv,
        device_id=device, device_id_type=MESH,
    )


def reduce_part(
    n_ha, n_wa, pc, sums_copy,
    sums, tables_h, tables_w, cotangent, tables_all,
    sums_in, tables_h_in, tables_w_in, partial, partial_in, slice_out, slice_in,
    h_send, h_recv, w_send, w_recv,
    own_send, own_recv, below_send, below_recv, slice_send, slice_recv, all_send, all_recv,
):
    r = lax.axis_index("ha")
    w = lax.axis_index("wa")
    kc = pc * n_wa
    has_next = r + 1 < n_ha
    has_prev = r > 0
    lanes = sums.shape[0]
    rows_h = tables_h.shape[1]
    rows_w = tables_w.shape[1]
    per_h = rows_h // STRIDE
    per_w = rows_w // STRIDE
    blocks = pc + kc - 1

    def meets_h(source, owner):
        return (per_h * owner + per_h > source) & (per_h * owner < source + n_ha)

    def meets_w(owner):
        return (per_w * owner + per_w > pc * w) & (per_w * owner < pc * w + blocks)

    def h_copy(target, slot):
        return remote(
            tables_h.at[target], tables_h_in.at[slot], h_send.at[target], h_recv.at[slot],
            (target, w),
        )

    def w_copy(target, slot):
        return remote(
            tables_w.at[target], tables_w_in.at[slot], w_send.at[target], w_recv.at[slot],
            (target, w),
        )

    @pl.loop(1, n_ha)
    def _(d):
        target = lax.rem(r + d, n_ha)

        @pl.when(meets_h(r, target))
        def _():
            h_copy(target, r).start()

        @pl.when(meets_w(target))
        def _():
            w_copy(target, r).start()

    for t in range(lanes):
        sums_in[t, pl.ds(r, 1)] = sums[t, pl.ds(r, 1)]
    tables_h_in[pl.ds(r, 1)] = tables_h[pl.ds(r, 1)]
    tables_w_in[pl.ds(r, 1)] = tables_w[pl.ds(r, 1)]

    @pl.loop(1, n_ha)
    def _(d):
        source = lax.rem(r + n_ha - d, n_ha)
        for t in range(lanes):
            sums_copy(t, source, source).wait_recv()

    for t in range(lanes):
        partial[:, 128 * t : 128 * (t + 1)] = jnp.sum(sums_in[t].astype(F32), axis=0)

    def own_copy(target, slot):
        return remote(
            partial, partial_in.at[0, slot], own_send.at[target], own_recv.at[slot], (r, target)
        )

    def below_copy(target, slot):
        return remote(
            partial, partial_in.at[1, slot], below_send.at[target], below_recv.at[slot],
            (r - 1, target),
        )

    def slice_copy(target, slot):
        return remote(
            slice_out, slice_in.at[slot], slice_send.at[target], slice_recv.at[slot], (r, target)
        )

    for d in range(1, n_wa):
        own_copy(lax.rem(w + d, n_wa), w).start()

    @pl.when(has_prev)
    def _():
        for d in range(n_wa):
            below_copy(lax.rem(w + d, n_wa), w).start()

    @pl.loop(1, n_ha)
    def _(d):
        source = lax.rem(r + n_ha - d, n_ha)

        @pl.when(meets_h(source, r))
        def _():
            h_copy(source, source).wait_recv()

        @pl.when(meets_w(r))
        def _():
            w_copy(source, source).wait_recv()

    slice_out[0:rows_h] = jnp.sum(tables_h_in[...].astype(F32), axis=0)
    slice_out[rows_h:] = jnp.sum(tables_w_in[...].astype(F32), axis=0)

    for d in range(1, n_wa):
        slice_copy(lax.rem(w + d, n_wa), w).start()

    slice_in[pl.ds(w, 1)] = slice_out[...][None]
    partial_in[0, pl.ds(w, 1)] = partial[...][None]

    for d in range(1, n_wa):
        slice_copy(lax.rem(w + d, n_wa), lax.rem(w + n_wa - d, n_wa)).wait_recv()
    tables_all[pl.ds(r, 1)] = jnp.sum(slice_in[...], axis=0)[None].astype(BF16)

    def all_copy(target, slot):
        return remote(
            tables_all.at[slot], tables_all.at[slot], all_send.at[target], all_recv.at[slot],
            (target, w),
        )

    @pl.loop(1, n_ha)
    def _(d):
        all_copy(lax.rem(r + d, n_ha), r).start()

    @pl.when(jnp.logical_not(has_next))
    def _():
        partial_in[1] = jnp.zeros_like(partial_in[1])

    for d in range(1, n_wa):
        own_copy(lax.rem(w + d, n_wa), lax.rem(w + n_wa - d, n_wa)).wait_recv()

    @pl.when(has_next)
    def _():
        for d in range(n_wa):
            below_copy(lax.rem(w + d, n_wa), lax.rem(w + n_wa - d, n_wa)).wait_recv()

    width = cotangent.shape[-1]
    span = cotangent.shape[2]
    for side in range(2):
        whole = jnp.sum(partial_in[side], axis=0)
        for a in range(2):
            rows = whole[a * kc : (a + 1) * kc]
            chosen = None
            for c in range(n_wa):
                piece = rows[c * pc : min(kc, (c + 1) * pc + 1)]
                piece = jnp.concatenate(
                    [piece, jnp.zeros((span - piece.shape[0], width), F32)], 0
                )
                chosen = piece if chosen is None else jnp.where(w == c, piece, chosen)
            cotangent[side, a] = chosen

    @pl.loop(1, n_ha)
    def _(d):
        target = lax.rem(r + d, n_ha)
        for t in range(lanes):
            sums_copy(t, target, r).wait_send()

        @pl.when(meets_h(r, target))
        def _():
            h_copy(target, r).wait_send()

        @pl.when(meets_w(target))
        def _():
            w_copy(target, r).wait_send()

    for d in range(1, n_wa):
        target = lax.rem(w + d, n_wa)
        slice_copy(target, w).wait_send()
        own_copy(target, w).wait_send()

    @pl.when(has_prev)
    def _():
        for d in range(n_wa):
            below_copy(lax.rem(w + d, n_wa), w).wait_send()

    @pl.loop(1, n_ha)
    def _(d):
        source = lax.rem(r + n_ha - d, n_ha)
        all_copy(source, source).wait_recv()

    @pl.loop(1, n_ha)
    def _(d):
        all_copy(lax.rem(r + d, n_ha), r).wait_send()


def fused_kernel(
    n_ha, n_wa, pc, own_cols, tile_rows, rows_h,
    key_hbm, value_hbm, query_hbm, grad_hbm, key_kernel, value_kernel, height_table, width_table,
    query_out, cotangent, tables_all,
    queries, out_grad, query_grad, gathered, sums, tables_h, tables_w, sums_in, tables_h_in,
    tables_w_in, flat_h, flat_w, turned_h, turned_w, height_float, height_rows, width_rows, big_send, sums_send, sums_recv,
    *rest,
):
    gather_refs, attention_refs, reduce_refs = rest[:10], rest[10:22], rest[22:]
    r = lax.axis_index("ha")
    w = lax.axis_index("wa")
    kc = pc * n_wa
    blocks = pc + kc - 1
    fetch = [
        pltpu.make_async_copy(query_hbm, queries, big_send.at[0]),
        pltpu.make_async_copy(grad_hbm, out_grad, big_send.at[1]),
    ]
    tables_h_in[...] = jnp.zeros_like(tables_h_in)
    tables_w_in[...] = jnp.zeros_like(tables_w_in)

    def prepare():
        for copy in fetch:
            copy.start()
        for table, flat, turned in (
            (height_table, flat_h, turned_h),
            (width_table, flat_w, turned_w),
        ):
            flat[...] = jnp.zeros_like(flat)
            flat[:, : table.shape[1]] = table[...].astype(F32)
            turned[...] = flat[...].T
        for v in range(n_ha):
            start = pl.multiple_of(r * STRIDE + v * STRIDE, STRIDE)
            height_float[pl.ds(n_ha - 1 - v, STRIDE, stride=n_ha)] = turned_h[
                pl.ds(start, STRIDE)
            ]
        once = height_float[...]
        height_rows[...] = jnp.concatenate([once] * HEADS, 1).astype(BF16)
        for v in range(blocks):
            start = pl.multiple_of(w * own_cols + v * STRIDE, STRIDE)
            once = turned_w[pl.ds(start, STRIDE)]
            width_rows[(blocks - 1 - v) * STRIDE : (blocks - v) * STRIDE] = jnp.concatenate(
                [once] * HEADS, 1
            ).astype(BF16)

    gather_part(
        n_ha, n_wa, pc, key_hbm, value_hbm, key_kernel, value_kernel, gathered, *gather_refs,
        prepare,
    )
    for copy in fetch:
        copy.wait()

    def sums_copy(t, target, slot):
        return remote(
            sums.at[t, target], sums_in.at[t, slot], sums_send.at[t, target], sums_recv.at[t, slot],
            (target, w),
        )

    def send_lanes(t):
        @pl.loop(1, n_ha)
        def _(d):
            sums_copy(t, lax.rem(r + d, n_ha), r).start()

    attention_part(
        n_ha, n_wa, pc, own_cols, tile_rows, rows_h,
        queries, out_grad, gathered, height_rows, width_rows,
        query_grad, sums, tables_h, tables_w, send_lanes, *attention_refs,
    )
    put = pltpu.make_async_copy(query_grad, query_out, big_send.at[2])
    put.start()
    reduce_part(
        n_ha, n_wa, pc, sums_copy, sums, tables_h, tables_w, cotangent, tables_all,
        sums_in, tables_h_in, tables_w_in, *reduce_refs,
    )
    put.wait()


def fused(
    n_ha, n_wa, rows_h, rows_w,
    queries, key_tokens, value_tokens, out_grad, key_kernel, value_kernel, height_table, width_table,
):
    own_rows, own_cols, width = queries.shape
    pc = own_cols // STRIDE
    kc = pc * n_wa
    keys = n_ha * kc
    blocks = pc + kc - 1
    span = round_up(pc + 1, 8)
    lanes = width // 128
    entries = rows_h + rows_w
    tile_rows = max(1, min(own_rows, 256 // own_cols))
    tokens = own_rows * own_cols
    wide = max(window(head)[1] - window(head)[0] for head in range(HEADS))
    vmem = pl.BlockSpec(memory_space=pltpu.VMEM)
    anywhere = pl.BlockSpec(memory_space=pl.ANY)
    dma = pltpu.SemaphoreType.DMA
    ram = pltpu.VMEM
    return pl.pallas_call(
        functools.partial(fused_kernel, n_ha, n_wa, pc, own_cols, tile_rows, rows_h),
        out_shape=(
            jax.ShapeDtypeStruct((tokens, width), BF16),
            jax.ShapeDtypeStruct((2, 2, span, width), F32),
            jax.ShapeDtypeStruct((n_ha, entries, HD), BF16),
        ),
        in_specs=[anywhere] * 4 + [vmem] * 4,
        out_specs=(anywhere, vmem, vmem),
        scratch_shapes=[
            ram((tokens, width), BF16),
            ram((tokens, width), BF16),
            ram((tokens, width), BF16),
            ram((n_ha, 2 * kc, width), BF16),
            ram((lanes, n_ha, 2 * kc, 128), BF16),
            ram((n_ha, rows_h, HD), BF16),
            ram((n_ha, rows_w, HD), BF16),
            ram((lanes, n_ha, 2 * kc, 128), BF16),
            ram((n_ha, rows_h, HD), BF16),
            ram((n_ha, rows_w, HD), BF16),
            ram((HD, round_up(height_table.shape[1], 128)), F32),
            ram((HD, round_up(width_table.shape[1], 128)), F32),
            ram((round_up(height_table.shape[1], 128), HD), F32),
            ram((round_up(width_table.shape[1], 128), HD), F32),
            ram((own_rows * n_ha, HD), F32),
            ram((own_rows * n_ha, width), BF16),
            ram((blocks * STRIDE, width), BF16),
            dma((3,)),
            dma((lanes, n_ha)),
            dma((lanes, n_ha)),
            ram((2, 3, own_cols, width), BF16),
            ram((2, 2, span, width), F32),
            ram((2, n_wa, 2, span, width), F32),
            dma((4,)),
            dma((n_wa,)),
            dma((n_wa,)),
            dma((n_wa,)),
            dma((n_wa,)),
            dma((n_ha,)),
            dma((n_ha,)),
            ram((keys, wide), BF16),
            ram((keys, wide), BF16),
            ram((own_rows * n_ha, wide), BF16),
            ram((blocks * STRIDE, wide), BF16),
            ram((keys + blocks * STRIDE, wide), F32),
            ram((own_rows * n_ha, wide), F32),
            ram((keys, wide), F32),
            ram((keys, width), F32),
            ram((keys, width), F32),
            ram((own_rows * n_ha, width), F32),
            ram((blocks * STRIDE, width), F32),
            ram((own_rows * n_ha, HD), F32),
            ram((2 * kc, width), F32),
            ram((2, n_wa, 2 * kc, width), F32),
            ram((entries, HD), F32),
            ram((n_wa, entries, HD), F32),
        ]
        + [dma((n_ha,))] * 4
        + [dma((n_wa,))] * 6
        + [dma((n_ha,))] * 2,
        compiler_params=pltpu.CompilerParams(
            collective_id=0, has_side_effects=True, vmem_limit_bytes=56 * 2**20
        ),
        name="pooled_attention",
    )(
        key_tokens, value_tokens, queries.reshape(tokens, width), out_grad.reshape(tokens, width),
        key_kernel, value_kernel, height_table, width_table,
    )


def write_kernel(
    pc, rows_h, cotangent_hbm, tables_hbm, query_in, key_kernel, value_kernel,
    query_out, key_out, value_out, height, wide,
    middle, edges, cotangent, tables, loaded, done,
):
    width = edges.shape[-1]
    loads = [
        pltpu.make_async_copy(cotangent_hbm, cotangent, loaded.at[0]),
        pltpu.make_async_copy(tables_hbm, tables, loaded.at[1]),
    ]
    copies = [pltpu.make_async_copy(query_in, query_out, done.at[6])]
    for copy in loads + copies:
        copy.start()
    middle[...] = jnp.zeros_like(middle)
    for a, out in enumerate((key_out, value_out)):
        copies.append(
            pltpu.make_async_copy(middle, out.at[pl.ds(2, STRIDE - 3)], done.at[3 * a])
        )
        copies[-1].start()
    edges[...] = jnp.zeros_like(edges)
    loads[0].wait()
    at = lax.broadcasted_iota(jnp.int32, (STRIDE, 1), 0)
    for a, (kernel, out) in enumerate(((key_kernel, key_out), (value_kernel, value_out))):
        for row, tap, side in ((0, 1, 0), (1, 2, 0), (2, 0, 1)):
            taps = kernel[tap].astype(F32)
            for k in range(pc):
                here = cotangent[side, a, k : k + 1]
                after = cotangent[side, a, k + 1 : k + 2]
                block = jnp.where(
                    at == 0,
                    here * taps[1:2],
                    jnp.where(
                        at == 1,
                        here * taps[2:3],
                        jnp.where(at == STRIDE - 1, after * taps[0:1], jnp.zeros((STRIDE, width), F32)),
                    ),
                )
                edges[a, row, STRIDE * k : STRIDE * (k + 1)] = block.astype(BF16)
        copies.append(
            pltpu.make_async_copy(edges.at[a, pl.ds(0, 2)], out.at[pl.ds(0, 2)], done.at[3 * a + 1])
        )
        copies[-1].start()
        copies.append(
            pltpu.make_async_copy(
                edges.at[a, pl.ds(2, 1)], out.at[pl.ds(STRIDE - 1, 1)], done.at[3 * a + 2]
            )
        )
        copies[-1].start()
    loads[1].wait()
    n_ha = tables.shape[0]
    for out, first, last in ((height, 0, rows_h), (wide, rows_h, tables.shape[1])):
        value = tables[:, first:last].astype(F32).reshape(n_ha * (last - first), HD)
        out[...] = value.T[:, : out.shape[1]]
    for copy in copies:
        copy.wait()


def write_back(
    rows_h, cotangent, tables, query_grad, key_kernel, value_kernel, shape, heights, widths
):
    vmem = pl.BlockSpec(memory_space=pltpu.VMEM)
    anywhere = pl.BlockSpec(memory_space=pl.ANY)
    return pl.pallas_call(
        functools.partial(write_kernel, shape[1] // STRIDE, rows_h),
        out_shape=(
            jax.ShapeDtypeStruct(query_grad.shape, BF16),
            jax.ShapeDtypeStruct(shape, BF16),
            jax.ShapeDtypeStruct(shape, BF16),
            jax.ShapeDtypeStruct((HD, heights), F32),
            jax.ShapeDtypeStruct((HD, widths), F32),
        ),
        in_specs=[anywhere] * 3 + [vmem] * 2,
        out_specs=(anywhere,) * 3 + (vmem,) * 2,
        scratch_shapes=[
            pltpu.VMEM((STRIDE - 3,) + shape[1:], BF16),
            pltpu.VMEM((2, 3) + shape[1:], BF16),
            pltpu.VMEM(cotangent.shape, F32),
            pltpu.VMEM(tables.shape, BF16),
            pltpu.SemaphoreType.DMA((2,)),
            pltpu.SemaphoreType.DMA((7,)),
        ],
        compiler_params=pltpu.CompilerParams(vmem_limit_bytes=56 * 2**20),
        name="write_back",
    )(cotangent, tables, query_grad, key_kernel, value_kernel)


def on_device(
    queries, key_tokens, value_tokens, out_grad, key_kernel, value_kernel, height_table, width_table
):
    own_rows, own_cols, width = queries.shape
    n_ha = lax.axis_size("ha")
    n_wa = lax.axis_size("wa")
    assert own_rows == STRIDE and own_cols % STRIDE == 0
    heights = height_table.shape[0]
    widths = width_table.shape[0]
    rows_h = round_up(-(-heights // n_ha), STRIDE)
    rows_w = round_up(-(-widths // n_ha), STRIDE)
    query_grad, cotangent, tables_all = fused(
        n_ha, n_wa, rows_h, rows_w,
        queries, key_tokens, value_tokens, out_grad, key_kernel, value_kernel, height_table.T,
        width_table.T,
    )
    query_grad, key_grad, value_grad, height_grad, width_grad = write_back(
        rows_h, cotangent, tables_all, query_grad, key_kernel, value_kernel, queries.shape,
        heights, widths,
    )
    return (
        query_grad.reshape(queries.shape), key_grad, value_grad, height_grad.T, width_grad.T
    )


def solution(mesh):
    placed = (
        P("ha", "wa", None),
        P("ha", "wa", None),
        P("ha", "wa", None),
        P("ha", "wa", None),
        P(),
        P(),
        P(),
        P(),
    )
    return jax.shard_map(
        on_device,
        mesh=mesh,
        in_specs=placed,
        out_specs=(P("ha", "wa", None), P("ha", "wa", None), P("ha", "wa", None), P(), P()),
        check_vma=False,
    )
```

```python
import functools

import jax
import jax.numpy as jnp
from jax import lax
from jax.experimental import pallas as pl
from jax.experimental.pallas import tpu as pltpu
from jax.sharding import PartitionSpec as P

HEADS = 4
HD = 96
KS = 3
STRIDE = 16
MESH = pl.DeviceIdType.MESH
F32 = jnp.float32
BF16 = jnp.bfloat16


def round_up(value, unit):
    return -(-value // unit) * unit


def gather_part(
    n_ha, n_wa, pc,
    key_hbm, value_hbm, key_kernel, value_kernel, gathered,
    tokens, part, arrived, load_sem, own_send, own_recv, next_send, next_recv, row_send, row_recv, prepare,
):
    r = lax.axis_index("ha")
    w = lax.axis_index("wa")
    span = part.shape[2]
    kc = pc * n_wa
    last = tokens.shape[2] // pc
    has_next = r + 1 < n_ha
    has_prev = r > 0

    loads = []
    for a, source in enumerate((key_hbm, value_hbm)):
        loads.append(
            pltpu.make_async_copy(
                source.at[pl.ds(0, 2)], tokens.at[a, pl.ds(0, 2)], load_sem.at[2 * a]
            )
        )
        loads.append(
            pltpu.make_async_copy(
                source.at[pl.ds(STRIDE - 1, 1)], tokens.at[a, pl.ds(2, 1)], load_sem.at[2 * a + 1]
            )
        )
    for load in loads:
        load.start()

    barrier = pltpu.get_barrier_semaphore()

    @pl.loop(1, n_ha)
    def _(d):
        pl.semaphore_signal(
            barrier, 1, device_id=(lax.rem(r + d, n_ha), w), device_id_type=MESH
        )

    for d in range(1, n_wa):
        other = lax.rem(w + d, n_wa)
        pl.semaphore_signal(barrier, 1, device_id=(r, other), device_id_type=MESH)

        @pl.when(has_next)
        def _():
            pl.semaphore_signal(barrier, 1, device_id=(r + 1, other), device_id_type=MESH)

        @pl.when(has_prev)
        def _():
            pl.semaphore_signal(barrier, 1, device_id=(r - 1, other), device_id_type=MESH)

    extra = jnp.where(has_next, n_wa - 1, 0) + jnp.where(has_prev, n_wa - 1, 0)

    for load in loads:
        load.wait()

    def pooled(a, kernel, uses):
        rows = [None] * (pc + 1)

        def add(k, term):
            rows[k] = term if rows[k] is None else rows[k] + term

        for at, tap in uses:
            line = tokens[a, at].astype(F32)
            for k in range(pc):
                for col, to, key in ((0, 1, k), (1, 2, k), (STRIDE - 1, 0, k + 1)):
                    at_col = STRIDE * k + col
                    weight = kernel[tap, to : to + 1].astype(F32)
                    add(key, line[at_col : at_col + 1] * weight)
        return jnp.concatenate(
            rows + [jnp.zeros((span - pc - 1, tokens.shape[-1]), F32)], 0
        )

    for a, kernel in enumerate((key_kernel, value_kernel)):
        part[0, a] = pooled(a, kernel, ((0, 1), (1, 2)))
        part[1, a] = pooled(a, kernel, ((2, 0),))

    pl.semaphore_wait(barrier, n_ha - 1 + n_wa - 1 + extra)

    def own_copy(target, slot):
        return pltpu.make_async_remote_copy(
            src_ref=part.at[0],
            dst_ref=arrived.at[0, slot],
            send_sem=own_send.at[target],
            recv_sem=own_recv.at[slot],
            device_id=(r, target),
            device_id_type=MESH,
        )

    def next_copy(target, slot):
        return pltpu.make_async_remote_copy(
            src_ref=part.at[1],
            dst_ref=arrived.at[1, slot],
            send_sem=next_send.at[target],
            recv_sem=next_recv.at[slot],
            device_id=(r + 1, target),
            device_id_type=MESH,
        )

    for d in range(1, n_wa):
        own_copy(lax.rem(w + d, n_wa), w).start()

    @pl.when(has_next)
    def _():
        for d in range(n_wa):
            next_copy(lax.rem(w + d, n_wa), w).start()

    arrived[0, pl.ds(w, 1)] = part[0:1]
    prepare()

    @pl.when(r == 0)
    def _():
        arrived[1] = jnp.zeros_like(arrived[1])

    for d in range(1, n_wa):
        own_copy(lax.rem(w + d, n_wa), lax.rem(w + n_wa - d, n_wa)).wait_recv()

    @pl.when(has_prev)
    def _():
        for d in range(n_wa):
            next_copy(lax.rem(w + d, n_wa), lax.rem(w + n_wa - d, n_wa)).wait_recv()

    halves = []
    for a in range(2):
        blocks = []
        carried = None
        for c in range(n_wa):
            block = arrived[0, c, a] + arrived[1, c, a]
            if carried is not None:
                block = jnp.concatenate([block[0:1] + carried, block[1:]], 0)
            carried = block[pc : pc + 1]
            blocks.append(block[0:pc])
        halves.append(jnp.concatenate(blocks, 0))
    gathered[pl.ds(r, 1)] = jnp.concatenate(halves, 0).astype(BF16)[None]

    def row_copy(target, slot):
        return pltpu.make_async_remote_copy(
            src_ref=gathered.at[slot],
            dst_ref=gathered.at[slot],
            send_sem=row_send.at[target],
            recv_sem=row_recv.at[slot],
            device_id=(target, w),
            device_id_type=MESH,
        )

    @pl.loop(1, n_ha)
    def _(d):
        row_copy(lax.rem(r + d, n_ha), r).start()

    for d in range(1, n_wa):
        own_copy(lax.rem(w + d, n_wa), w).wait_send()

    @pl.when(has_next)
    def _():
        for d in range(n_wa):
            next_copy(lax.rem(w + d, n_wa), w).wait_send()

    @pl.loop(1, n_ha)
    def _(d):
        source = lax.rem(r + n_ha - d, n_ha)
        row_copy(source, source).wait_recv()

    @pl.loop(1, n_ha)
    def _(d):
        row_copy(lax.rem(r + d, n_ha), r).wait_send()


def window(head):
    low = head * HD // 128 * 128
    high = round_up((head + 1) * HD, 128)
    return low, high


def nt(left, right):
    return lax.dot_general(left, right, (((1,), (1,)), ((), ())), preferred_element_type=F32)


def nn(left, right):
    return lax.dot_general(left, right, (((1,), (0,)), ((), ())), preferred_element_type=F32)


def tn(left, right):
    return lax.dot_general(left, right, (((0,), (0,)), ((), ())), preferred_element_type=F32)


def attention_part(
    n_ha, n_wa, pc, own_cols, tile_rows, rows_h,
    queries, out_grad, gathered, height_rows, width_rows,
    query_grad, sums, tables_h, tables_w, send_lanes,
    key_win, value_win, height_win, width_win, main_acc, height_acc, value_acc,
    key_full, value_full, height_full, width_full, fold,
):
    kc = pc * n_wa
    kr = n_ha
    keys = kr * kc
    blocks = pc + kc - 1
    scale = HD ** (-0.5)
    tile = tile_rows * own_cols
    tiles = queries.shape[0] // tile
    hrows = tile_rows * kr

    lane = lax.broadcasted_iota(jnp.int32, (1, tile), 1)
    lane_row = lane // own_cols
    lane_col = lane % own_cols
    lane_block = lane_col // STRIDE
    lane_in = lane_col % STRIDE
    in_block = lax.broadcasted_iota(jnp.int32, (1, STRIDE, tile), 1) == lane_in[None]

    for head in range(HEADS):
        low, high = window(head)
        size = high - low
        channel = lax.broadcasted_iota(jnp.int32, (1, size), 1) + low
        mine = (channel >= head * HD) & (channel < (head + 1) * HD)
        zero = jnp.zeros((), BF16)

        pooled = gathered[:, :, low:high].astype(F32)
        pooled = jnp.where(mine[None], pooled, 0.0)
        key_win[:, :size] = pooled[:, :kc].reshape(keys, size).astype(BF16)
        value_win[:, :size] = pooled[:, kc:].reshape(keys, size).astype(BF16)
        height_win[:, :size] = jnp.where(mine, height_rows[:, low:high].astype(F32), 0.0).astype(
            BF16
        )
        width_win[:, :size] = jnp.where(mine, width_rows[:, low:high].astype(F32), 0.0).astype(BF16)

        def step(i, first):
            base = pl.multiple_of(i * tile, tile)
            hbase = pl.multiple_of(i * hrows, hrows)
            q = queries[pl.ds(base, tile), low:high]
            g = out_grad[pl.ds(base, tile), low:high]
            kw_ = key_win[:, :size]
            vw_ = value_win[:, :size]
            hw_ = height_win[pl.ds(hbase, hrows), :size]
            ww_ = width_win[:, :size]
            raw = nt(jnp.concatenate([kw_, ww_, hw_], 0), q)
            raw_w = raw[keys : keys + blocks * STRIDE]
            raw_h = raw[keys + blocks * STRIDE :]
            rel_h = raw_h[0:kr]
            for a in range(1, tile_rows):
                rel_h = jnp.where(lane_row == a, raw_h[a * kr : (a + 1) * kr], rel_h)
            picked = jnp.sum(
                jnp.where(in_block, raw_w.reshape(blocks, STRIDE, tile), 0.0), axis=1
            )
            rel_w = picked[pc - 1 : pc - 1 + kc]
            for u in range(1, pc):
                rel_w = jnp.where(lane_block == u, picked[pc - 1 - u : pc - 1 - u + kc], rel_w)
            scores = raw[:keys].reshape(kr, kc, tile) * scale + (rel_h[:, None, :] + rel_w[None])
            top = jnp.max(jnp.max(scores, axis=0), axis=0, keepdims=True)
            weights = jnp.exp(scores - top[None])
            total = jnp.sum(jnp.sum(weights, axis=0), axis=0, keepdims=True)
            probs = weights * (1.0 / total)[None]
            probs_low = probs.astype(BF16)
            grad_probs = nt(vw_, g).reshape(kr, kc, tile)
            delta = jnp.sum(
                jnp.sum(probs_low.astype(F32) * grad_probs, axis=0), axis=0, keepdims=True
            )
            grad_scores = probs * (grad_probs - delta[None])
            grad_low = grad_scores.astype(BF16).reshape(keys, tile)
            probs_low = probs_low.reshape(keys, tile)
            grad_h = jnp.sum(grad_scores, axis=1)
            grad_w = jnp.sum(grad_scores, axis=0)
            spread_h = jnp.concatenate(
                [jnp.where(lane_row == a, grad_h, 0.0) for a in range(tile_rows)], 0
            ).astype(BF16)
            shifted = None
            for u in range(pc):
                pieces = []
                if pc - 1 - u:
                    pieces.append(jnp.zeros((pc - 1 - u, tile), F32))
                pieces.append(jnp.where(lane_block == u, grad_w, 0.0))
                if u:
                    pieces.append(jnp.zeros((u, tile), F32))
                piece = jnp.concatenate(pieces, 0)
                shifted = piece if shifted is None else shifted + piece
            spread_w = (
                jnp.where(in_block, shifted[:, None, :], 0.0)
                .reshape(blocks * STRIDE, tile)
                .astype(BF16)
            )
            d_query = tn(grad_low, kw_) * scale + tn(
                jnp.concatenate([spread_h, spread_w], 0), jnp.concatenate([hw_, ww_], 0)
            )
            old = query_grad[pl.ds(base, tile), low:high]
            query_grad[pl.ds(base, tile), low:high] = jnp.where(
                mine, d_query, old.astype(F32)
            ).astype(BF16)
            by_query = nn(jnp.concatenate([grad_low, spread_w, spread_h], 0), q)
            by_grad = nn(probs_low, g)
            split = keys + blocks * STRIDE
            if first:
                main_acc[:, :size] = by_query[:split]
                value_acc[:, :size] = by_grad
            else:
                main_acc[:, :size] += by_query[:split]
                value_acc[:, :size] += by_grad
            height_acc[pl.ds(hbase, hrows), :size] = by_query[split:]

        if head == 0:
            query_grad[...] = jnp.zeros_like(query_grad)
        step(0, True)
        if tiles > 1:

            @pl.loop(1, tiles, unroll=tiles - 1 if keys <= 256 else 1)
            def _(i):
                step(i, False)

        def merge(full, value):
            if head == 0:
                full[:, low:high] = value
            else:
                full[:, low:high] = jnp.where(mine, value, full[:, low:high])

        merge(key_full, main_acc[:keys, :size] * scale)
        merge(value_full, value_acc[:, :size])
        merge(width_full, main_acc[keys:, :size])
        merge(height_full, height_acc[:, :size])
        for t in range(queries.shape[1] // 128):
            if head == -(-128 * (t + 1) // HD) - 1:
                lanes = slice(128 * t, 128 * (t + 1))
                sums[t] = jnp.concatenate(
                    [
                        key_full[:, lanes].reshape(kr, kc, 128),
                        value_full[:, lanes].reshape(kr, kc, 128),
                    ],
                    1,
                ).astype(BF16)
                send_lanes(t)

    def folded(full):
        value = full[:, 0:HD]
        for head in range(1, HEADS):
            value = value + full[:, head * HD : (head + 1) * HD]
        return value

    tables_h[...] = jnp.zeros_like(tables_h)
    tables_w[...] = jnp.zeros_like(tables_w)
    r = lax.axis_index("ha")
    w = lax.axis_index("wa")
    fold[...] = folded(height_full)
    per_h = rows_h // STRIDE
    for kh in range(kr):
        at = r + (kr - 1 - kh)
        tables_h[at // per_h, pl.ds(pl.multiple_of((at % per_h) * STRIDE, STRIDE), STRIDE)] = fold[
            pl.ds(kh, STRIDE, stride=kr)
        ].astype(BF16)
    by_width = folded(width_full)
    per_w = tables_w.shape[1] // STRIDE
    for v in range(blocks):
        at = w * pc + (blocks - 1 - v)
        tables_w[at // per_w, pl.ds(pl.multiple_of((at % per_w) * STRIDE, STRIDE), STRIDE)] = (
            by_width[v * STRIDE : (v + 1) * STRIDE].astype(BF16)
        )


def remote(source, target, send, recv, device):
    return pltpu.make_async_remote_copy(
        src_ref=source, dst_ref=target, send_sem=send, recv_sem=recv,
        device_id=device, device_id_type=MESH,
    )


def reduce_part(
    n_ha, n_wa, pc, sums_copy,
    sums, tables_h, tables_w, cotangent, tables_all,
    sums_in, tables_h_in, tables_w_in, partial, partial_in, slice_out, slice_in,
    h_send, h_recv, w_send, w_recv,
    own_send, own_recv, below_send, below_recv, slice_send, slice_recv, all_send, all_recv,
):
    r = lax.axis_index("ha")
    w = lax.axis_index("wa")
    kc = pc * n_wa
    has_next = r + 1 < n_ha
    has_prev = r > 0
    lanes = sums.shape[0]
    rows_h = tables_h.shape[1]
    rows_w = tables_w.shape[1]
    per_h = rows_h // STRIDE
    per_w = rows_w // STRIDE
    blocks = pc + kc - 1

    def meets_h(source, owner):
        return (per_h * owner + per_h > source) & (per_h * owner < source + n_ha)

    def meets_w(owner):
        return (per_w * owner + per_w > pc * w) & (per_w * owner < pc * w + blocks)

    def h_copy(target, slot):
        return remote(
            tables_h.at[target], tables_h_in.at[slot], h_send.at[target], h_recv.at[slot],
            (target, w),
        )

    def w_copy(target, slot):
        return remote(
            tables_w.at[target], tables_w_in.at[slot], w_send.at[target], w_recv.at[slot],
            (target, w),
        )

    @pl.loop(1, n_ha)
    def _(d):
        target = lax.rem(r + d, n_ha)

        @pl.when(meets_h(r, target))
        def _():
            h_copy(target, r).start()

        @pl.when(meets_w(target))
        def _():
            w_copy(target, r).start()

    for t in range(lanes):
        sums_in[t, pl.ds(r, 1)] = sums[t, pl.ds(r, 1)]
    tables_h_in[pl.ds(r, 1)] = tables_h[pl.ds(r, 1)]
    tables_w_in[pl.ds(r, 1)] = tables_w[pl.ds(r, 1)]

    @pl.loop(1, n_ha)
    def _(d):
        source = lax.rem(r + n_ha - d, n_ha)
        for t in range(lanes):
            sums_copy(t, source, source).wait_recv()

    for t in range(lanes):
        partial[:, 128 * t : 128 * (t + 1)] = jnp.sum(sums_in[t].astype(F32), axis=0)

    def own_copy(target, slot):
        return remote(
            partial, partial_in.at[0, slot], own_send.at[target], own_recv.at[slot], (r, target)
        )

    def below_copy(target, slot):
        return remote(
            partial, partial_in.at[1, slot], below_send.at[target], below_recv.at[slot],
            (r - 1, target),
        )

    def slice_copy(target, slot):
        return remote(
            slice_out, slice_in.at[slot], slice_send.at[target], slice_recv.at[slot], (r, target)
        )

    for d in range(1, n_wa):
        own_copy(lax.rem(w + d, n_wa), w).start()

    @pl.when(has_prev)
    def _():
        for d in range(n_wa):
            below_copy(lax.rem(w + d, n_wa), w).start()

    @pl.loop(1, n_ha)
    def _(d):
        source = lax.rem(r + n_ha - d, n_ha)

        @pl.when(meets_h(source, r))
        def _():
            h_copy(source, source).wait_recv()

        @pl.when(meets_w(r))
        def _():
            w_copy(source, source).wait_recv()

    slice_out[0:rows_h] = jnp.sum(tables_h_in[...].astype(F32), axis=0)
    slice_out[rows_h:] = jnp.sum(tables_w_in[...].astype(F32), axis=0)

    for d in range(1, n_wa):
        slice_copy(lax.rem(w + d, n_wa), w).start()

    slice_in[pl.ds(w, 1)] = slice_out[...][None]
    partial_in[0, pl.ds(w, 1)] = partial[...][None]

    for d in range(1, n_wa):
        slice_copy(lax.rem(w + d, n_wa), lax.rem(w + n_wa - d, n_wa)).wait_recv()
    tables_all[pl.ds(r, 1)] = jnp.sum(slice_in[...], axis=0)[None].astype(BF16)

    def all_copy(target, slot):
        return remote(
            tables_all.at[slot], tables_all.at[slot], all_send.at[target], all_recv.at[slot],
            (target, w),
        )

    @pl.loop(1, n_ha)
    def _(d):
        all_copy(lax.rem(r + d, n_ha), r).start()

    @pl.when(jnp.logical_not(has_next))
    def _():
        partial_in[1] = jnp.zeros_like(partial_in[1])

    for d in range(1, n_wa):
        own_copy(lax.rem(w + d, n_wa), lax.rem(w + n_wa - d, n_wa)).wait_recv()

    @pl.when(has_next)
    def _():
        for d in range(n_wa):
            below_copy(lax.rem(w + d, n_wa), lax.rem(w + n_wa - d, n_wa)).wait_recv()

    width = cotangent.shape[-1]
    span = cotangent.shape[2]
    for side in range(2):
        whole = jnp.sum(partial_in[side], axis=0)
        for a in range(2):
            rows = whole[a * kc : (a + 1) * kc]
            chosen = None
            for c in range(n_wa):
                piece = rows[c * pc : min(kc, (c + 1) * pc + 1)]
                piece = jnp.concatenate(
                    [piece, jnp.zeros((span - piece.shape[0], width), F32)], 0
                )
                chosen = piece if chosen is None else jnp.where(w == c, piece, chosen)
            cotangent[side, a] = chosen

    @pl.loop(1, n_ha)
    def _(d):
        target = lax.rem(r + d, n_ha)
        for t in range(lanes):
            sums_copy(t, target, r).wait_send()

        @pl.when(meets_h(r, target))
        def _():
            h_copy(target, r).wait_send()

        @pl.when(meets_w(target))
        def _():
            w_copy(target, r).wait_send()

    for d in range(1, n_wa):
        target = lax.rem(w + d, n_wa)
        slice_copy(target, w).wait_send()
        own_copy(target, w).wait_send()

    @pl.when(has_prev)
    def _():
        for d in range(n_wa):
            below_copy(lax.rem(w + d, n_wa), w).wait_send()

    @pl.loop(1, n_ha)
    def _(d):
        source = lax.rem(r + n_ha - d, n_ha)
        all_copy(source, source).wait_recv()

    @pl.loop(1, n_ha)
    def _(d):
        all_copy(lax.rem(r + d, n_ha), r).wait_send()


def fused_kernel(
    n_ha, n_wa, pc, own_cols, tile_rows, rows_h,
    key_hbm, value_hbm, query_hbm, grad_hbm, key_kernel, value_kernel, height_table, width_table,
    query_out, cotangent, tables_all,
    queries, out_grad, query_grad, gathered, sums, tables_h, tables_w, sums_in, tables_h_in,
    tables_w_in, flat_h, flat_w, turned_h, turned_w, height_float, height_rows, width_rows, big_send, sums_send, sums_recv,
    *rest,
):
    gather_refs, attention_refs, reduce_refs = rest[:10], rest[10:22], rest[22:]
    r = lax.axis_index("ha")
    w = lax.axis_index("wa")
    kc = pc * n_wa
    blocks = pc + kc - 1
    fetch = [
        pltpu.make_async_copy(query_hbm, queries, big_send.at[0]),
        pltpu.make_async_copy(grad_hbm, out_grad, big_send.at[1]),
    ]
    tables_h_in[...] = jnp.zeros_like(tables_h_in)
    tables_w_in[...] = jnp.zeros_like(tables_w_in)

    def prepare():
        for copy in fetch:
            copy.start()
        for table, flat, turned in (
            (height_table, flat_h, turned_h),
            (width_table, flat_w, turned_w),
        ):
            flat[...] = jnp.zeros_like(flat)
            flat[:, : table.shape[1]] = table[...].astype(F32)
            turned[...] = flat[...].T
        for v in range(n_ha):
            start = pl.multiple_of(r * STRIDE + v * STRIDE, STRIDE)
            height_float[pl.ds(n_ha - 1 - v, STRIDE, stride=n_ha)] = turned_h[
                pl.ds(start, STRIDE)
            ]
        once = height_float[...]
        height_rows[...] = jnp.concatenate([once] * HEADS, 1).astype(BF16)
        for v in range(blocks):
            start = pl.multiple_of(w * own_cols + v * STRIDE, STRIDE)
            once = turned_w[pl.ds(start, STRIDE)]
            width_rows[(blocks - 1 - v) * STRIDE : (blocks - v) * STRIDE] = jnp.concatenate(
                [once] * HEADS, 1
            ).astype(BF16)

    gather_part(
        n_ha, n_wa, pc, key_hbm, value_hbm, key_kernel, value_kernel, gathered, *gather_refs,
        prepare,
    )
    for copy in fetch:
        copy.wait()

    def sums_copy(t, target, slot):
        return remote(
            sums.at[t, target], sums_in.at[t, slot], sums_send.at[t, target], sums_recv.at[t, slot],
            (target, w),
        )

    def send_lanes(t):
        @pl.loop(1, n_ha)
        def _(d):
            sums_copy(t, lax.rem(r + d, n_ha), r).start()

    attention_part(
        n_ha, n_wa, pc, own_cols, tile_rows, rows_h,
        queries, out_grad, gathered, height_rows, width_rows,
        query_grad, sums, tables_h, tables_w, send_lanes, *attention_refs,
    )
    put = pltpu.make_async_copy(query_grad, query_out, big_send.at[2])
    put.start()
    reduce_part(
        n_ha, n_wa, pc, sums_copy, sums, tables_h, tables_w, cotangent, tables_all,
        sums_in, tables_h_in, tables_w_in, *reduce_refs,
    )
    put.wait()


def fused(
    n_ha, n_wa, rows_h, rows_w,
    queries, key_tokens, value_tokens, out_grad, key_kernel, value_kernel, height_table, width_table,
):
    own_rows, own_cols, width = queries.shape
    pc = own_cols // STRIDE
    kc = pc * n_wa
    keys = n_ha * kc
    blocks = pc + kc - 1
    span = round_up(pc + 1, 8)
    lanes = width // 128
    entries = rows_h + rows_w
    tile_rows = max(1, min(own_rows, 256 // own_cols))
    tokens = own_rows * own_cols
    wide = max(window(head)[1] - window(head)[0] for head in range(HEADS))
    vmem = pl.BlockSpec(memory_space=pltpu.VMEM)
    anywhere = pl.BlockSpec(memory_space=pl.ANY)
    dma = pltpu.SemaphoreType.DMA
    ram = pltpu.VMEM
    return pl.pallas_call(
        functools.partial(fused_kernel, n_ha, n_wa, pc, own_cols, tile_rows, rows_h),
        out_shape=(
            jax.ShapeDtypeStruct((tokens, width), BF16),
            jax.ShapeDtypeStruct((2, 2, span, width), F32),
            jax.ShapeDtypeStruct((n_ha, entries, HD), BF16),
        ),
        in_specs=[anywhere] * 4 + [vmem] * 4,
        out_specs=(anywhere, vmem, vmem),
        scratch_shapes=[
            ram((tokens, width), BF16),
            ram((tokens, width), BF16),
            ram((tokens, width), BF16),
            ram((n_ha, 2 * kc, width), BF16),
            ram((lanes, n_ha, 2 * kc, 128), BF16),
            ram((n_ha, rows_h, HD), BF16),
            ram((n_ha, rows_w, HD), BF16),
            ram((lanes, n_ha, 2 * kc, 128), BF16),
            ram((n_ha, rows_h, HD), BF16),
            ram((n_ha, rows_w, HD), BF16),
            ram((HD, round_up(height_table.shape[1], 128)), F32),
            ram((HD, round_up(width_table.shape[1], 128)), F32),
            ram((round_up(height_table.shape[1], 128), HD), F32),
            ram((round_up(width_table.shape[1], 128), HD), F32),
            ram((own_rows * n_ha, HD), F32),
            ram((own_rows * n_ha, width), BF16),
            ram((blocks * STRIDE, width), BF16),
            dma((3,)),
            dma((lanes, n_ha)),
            dma((lanes, n_ha)),
            ram((2, 3, own_cols, width), BF16),
            ram((2, 2, span, width), F32),
            ram((2, n_wa, 2, span, width), F32),
            dma((4,)),
            dma((n_wa,)),
            dma((n_wa,)),
            dma((n_wa,)),
            dma((n_wa,)),
            dma((n_ha,)),
            dma((n_ha,)),
            ram((keys, wide), BF16),
            ram((keys, wide), BF16),
            ram((own_rows * n_ha, wide), BF16),
            ram((blocks * STRIDE, wide), BF16),
            ram((keys + blocks * STRIDE, wide), F32),
            ram((own_rows * n_ha, wide), F32),
            ram((keys, wide), F32),
            ram((keys, width), F32),
            ram((keys, width), F32),
            ram((own_rows * n_ha, width), F32),
            ram((blocks * STRIDE, width), F32),
            ram((own_rows * n_ha, HD), F32),
            ram((2 * kc, width), F32),
            ram((2, n_wa, 2 * kc, width), F32),
            ram((entries, HD), F32),
            ram((n_wa, entries, HD), F32),
        ]
        + [dma((n_ha,))] * 4
        + [dma((n_wa,))] * 6
        + [dma((n_ha,))] * 2,
        compiler_params=pltpu.CompilerParams(
            collective_id=0, has_side_effects=True, vmem_limit_bytes=56 * 2**20
        ),
        name="pooled_attention",
    )(
        key_tokens, value_tokens, queries.reshape(tokens, width), out_grad.reshape(tokens, width),
        key_kernel, value_kernel, height_table, width_table,
    )


def write_kernel(
    pc, rows_h, cotangent_hbm, tables_hbm, query_in, key_kernel, value_kernel,
    query_out, key_out, value_out, height, wide,
    middle, edges, cotangent, tables, passed, loaded, done,
):
    width = edges.shape[-1]
    loads = [
        pltpu.make_async_copy(cotangent_hbm, cotangent, loaded.at[0]),
        pltpu.make_async_copy(tables_hbm, tables, loaded.at[1]),
        pltpu.make_async_copy(query_in, passed, loaded.at[2]),
    ]
    copies = []
    for copy in loads:
        copy.start()
    middle[...] = jnp.zeros_like(middle)
    for a, out in enumerate((key_out, value_out)):
        copies.append(
            pltpu.make_async_copy(middle, out.at[pl.ds(2, STRIDE - 3)], done.at[3 * a])
        )
        copies[-1].start()
    edges[...] = jnp.zeros_like(edges)
    loads[0].wait()
    at = lax.broadcasted_iota(jnp.int32, (STRIDE, 1), 0)
    for a, (kernel, out) in enumerate(((key_kernel, key_out), (value_kernel, value_out))):
        for row, tap, side in ((0, 1, 0), (1, 2, 0), (2, 0, 1)):
            taps = kernel[tap].astype(F32)
            for k in range(pc):
                here = cotangent[side, a, k : k + 1]
                after = cotangent[side, a, k + 1 : k + 2]
                block = jnp.where(
                    at == 0,
                    here * taps[1:2],
                    jnp.where(
                        at == 1,
                        here * taps[2:3],
                        jnp.where(at == STRIDE - 1, after * taps[0:1], jnp.zeros((STRIDE, width), F32)),
                    ),
                )
                edges[a, row, STRIDE * k : STRIDE * (k + 1)] = block.astype(BF16)
        copies.append(
            pltpu.make_async_copy(edges.at[a, pl.ds(0, 2)], out.at[pl.ds(0, 2)], done.at[3 * a + 1])
        )
        copies[-1].start()
        copies.append(
            pltpu.make_async_copy(
                edges.at[a, pl.ds(2, 1)], out.at[pl.ds(STRIDE - 1, 1)], done.at[3 * a + 2]
            )
        )
        copies[-1].start()
    loads[2].wait()
    copies.append(pltpu.make_async_copy(passed, query_out, done.at[6]))
    copies[-1].start()
    loads[1].wait()
    n_ha = tables.shape[0]
    for out, first, last in ((height, 0, rows_h), (wide, rows_h, tables.shape[1])):
        value = tables[:, first:last].astype(F32).reshape(n_ha * (last - first), HD)
        out[...] = value.T[:, : out.shape[1]]
    for copy in copies:
        copy.wait()


def write_back(
    rows_h, cotangent, tables, query_grad, key_kernel, value_kernel, shape, heights, widths
):
    vmem = pl.BlockSpec(memory_space=pltpu.VMEM)
    anywhere = pl.BlockSpec(memory_space=pl.ANY)
    return pl.pallas_call(
        functools.partial(write_kernel, shape[1] // STRIDE, rows_h),
        out_shape=(
            jax.ShapeDtypeStruct(query_grad.shape, BF16),
            jax.ShapeDtypeStruct(shape, BF16),
            jax.ShapeDtypeStruct(shape, BF16),
            jax.ShapeDtypeStruct((HD, heights), F32),
            jax.ShapeDtypeStruct((HD, widths), F32),
        ),
        in_specs=[anywhere] * 3 + [vmem] * 2,
        out_specs=(anywhere,) * 3 + (vmem,) * 2,
        scratch_shapes=[
            pltpu.VMEM((STRIDE - 3,) + shape[1:], BF16),
            pltpu.VMEM((2, 3) + shape[1:], BF16),
            pltpu.VMEM(cotangent.shape, F32),
            pltpu.VMEM(tables.shape, BF16),
            pltpu.VMEM(query_grad.shape, BF16),
            pltpu.SemaphoreType.DMA((3,)),
            pltpu.SemaphoreType.DMA((7,)),
        ],
        compiler_params=pltpu.CompilerParams(vmem_limit_bytes=56 * 2**20),
        name="write_back",
    )(cotangent, tables, query_grad, key_kernel, value_kernel)


def on_device(
    queries, key_tokens, value_tokens, out_grad, key_kernel, value_kernel, height_table, width_table
):
    own_rows, own_cols, width = queries.shape
    n_ha = lax.axis_size("ha")
    n_wa = lax.axis_size("wa")
    assert own_rows == STRIDE and own_cols % STRIDE == 0
    heights = height_table.shape[0]
    widths = width_table.shape[0]
    rows_h = round_up(-(-heights // n_ha), STRIDE)
    rows_w = round_up(-(-widths // n_ha), STRIDE)
    query_grad, cotangent, tables_all = fused(
        n_ha, n_wa, rows_h, rows_w,
        queries, key_tokens, value_tokens, out_grad, key_kernel, value_kernel, height_table.T,
        width_table.T,
    )
    query_grad, key_grad, value_grad, height_grad, width_grad = write_back(
        rows_h, cotangent, tables_all, query_grad, key_kernel, value_kernel, queries.shape,
        heights, widths,
    )
    return (
        query_grad.reshape(queries.shape), key_grad, value_grad, height_grad.T, width_grad.T
    )


def solution(mesh):
    placed = (
        P("ha", "wa", None),
        P("ha", "wa", None),
        P("ha", "wa", None),
        P("ha", "wa", None),
        P(),
        P(),
        P(),
        P(),
    )
    return jax.shard_map(
        on_device,
        mesh=mesh,
        in_specs=placed,
        out_specs=(P("ha", "wa", None), P("ha", "wa", None), P("ha", "wa", None), P(), P()),
        check_vma=False,
    )
```
